512 devices in a mesh: seq: 8 (over z_hi, x), chan: 64 (over z_lo, y, core).
Axes of the slice: x: 4, y: 4, z: 16 (z_hi: 2, z_lo: 8; z = z_hi * 8 + z_lo), core: 2. Of those that a mesh axis runs over, the one named last changes fastest.
Arguments:
- query_gate: bfloat16 [1024, 8192], P('chan', 'seq'), may hold values from -6 to 6
- key_gate: bfloat16 [1024, 8192], P('chan', 'seq'), may hold values from -6 to 6
- values: bfloat16 [1024, 8192], P('chan', 'seq'), may hold values from -6 to 6
- filters: float32 [256, 8192], P(None, ('seq', 'chan')), may hold values from -2 to 2
- out_grad: bfloat16 [1024, 8192], P('chan', 'seq'), may hold values from -6 to 6
Outputs:
- query_grad: bfloat16 [1024, 8192], P('chan', 'seq')
- key_grad: bfloat16 [1024, 8192], P('chan', 'seq')
- value_grad: bfloat16 [1024, 8192], P('chan', 'seq')
- filter_grad: float32 [256, 8192], P(None, ('seq', 'chan'))
The draws below stay inside these ranges and needn't reach their ends.
All inputs are finite; a program needn't handle non-finite values.
Results may differ from the reference program's by a relative error of at most 0.0019.
Values sent between devices are 32-bit elements; how exact they have to be, the bound alone decides.
No kernel may reach another device: no remote copies, remote signals or barrier semaphores. Data moves between devices by JAX's collectives and lax.ppermute only.
A program may use at most 128 MiB of HBM per device.

```python
import jax
import jax.numpy as jnp
from jax import lax

CHANNELS = 1024
FILTERS = 256
SEQ_LEN = 8192


def draw_filters(key, part):
    key = jax.random.fold_in(key, 11)
    key_kind, key_fast, key_slow, key_noise = jax.random.split(key, 4)
    positions = jnp.arange(SEQ_LEN, dtype=jnp.float32)[None, :]
    slow_share = 0.5
    noise_vals = jnp.clip(jax.random.normal(key_noise, (FILTERS, SEQ_LEN), jnp.float32), -4.0, 4.0)
    picker = jax.random.uniform(key_kind, (FILTERS, 1), jnp.float32)
    fast_rate = jnp.exp(jax.random.uniform(key_fast, (FILTERS, 1), jnp.float32, jnp.log(1.0 / 50.0), jnp.log(1.0 / 30.0)))
    slow_rate = jnp.exp(jax.random.uniform(key_slow, (FILTERS, 1), jnp.float32, jnp.log(0.3 / SEQ_LEN), jnp.log(2.0 / SEQ_LEN)))
    decay_rate = jnp.where(picker < slow_share, slow_rate, fast_rate)
    amplitude = jnp.sqrt(2.0 * decay_rate / (1.0 - jnp.exp(-2.0 * decay_rate * SEQ_LEN)))
    return (noise_vals * amplitude * jnp.exp(-decay_rate * positions)).astype(jnp.float32)


def level_of(own_key, dims, cuts, least, high):
    level = 1.0
    for position, shards_of in cuts:
        heights = jax.random.uniform(jax.random.fold_in(jax.random.fold_in(own_key, 6), position), (shards_of,), jnp.float32, least / len(cuts), high / len(cuts))
        level = level * jnp.repeat(jnp.exp(heights), dims[position] // shards_of).reshape((-1,) + (1,) * (len(dims) - 1 - position))
    return level


def noise(own_key, shape, width, most, pieces=(), kind=jnp.bfloat16):
    result = width * jax.random.normal(own_key, shape, jnp.float32)
    if pieces:
        result = result * level_of(own_key, shape, pieces, -0.22, 0.18)
    return jnp.clip(result, -most, most).astype(kind)


def setup_inputs(seed: int = 0) -> dict:
    keys = jax.random.split(jax.random.key(seed), 6)
    return {
        "query_gate": noise(keys[0], (CHANNELS, SEQ_LEN), 1.0, 6.0, ((0, 64), (1, 8))),
        "key_gate": noise(keys[1], (CHANNELS, SEQ_LEN), 1.0, 6.0, ((0, 64), (1, 8))),
        "values": noise(keys[2], (CHANNELS, SEQ_LEN), 1.0, 6.0, ((0, 64), (1, 8))),
        "filters": draw_filters(jax.random.fold_in(keys[5], 71), 0),
        "out_grad": noise(keys[4], (CHANNELS, SEQ_LEN), 1.0, 6.0, ((0, 64), (1, 8))),
    }


def reference(query_gate, key_gate, values, filters, out_grad):
    channel_count, seq_len = query_gate.shape
    filter_count = filters.shape[0]
    group_count = channel_count // filter_count
    full_len = 2 * seq_len
    filter_spec = jnp.fft.rfft(filters, n=full_len, axis=-1)

    def regrouped(array):
        return array.reshape(group_count, filter_count, seq_len)

    def one_group(running_sum, inputs):
        query_part, key_part, value_part, grad_part = inputs
        gate_in = key_part.astype(jnp.float32) * value_part.astype(jnp.float32)
        grad_conv = grad_part.astype(jnp.float32) * query_part.astype(jnp.float32)
        gate_spec = jnp.fft.rfft(gate_in, n=full_len, axis=-1)
        grad_spec = jnp.fft.rfft(grad_conv, n=full_len, axis=-1)
        conv_out = jnp.fft.irfft(gate_spec * filter_spec, n=full_len, axis=-1)[:, :seq_len]
        grad_in = jnp.fft.irfft(grad_spec * jnp.conj(filter_spec), n=full_len, axis=-1)[:, :seq_len]
        filter_terms = jnp.fft.irfft(grad_spec * jnp.conj(gate_spec), n=full_len, axis=-1)[:, :seq_len]
        query_out = (grad_part.astype(jnp.float32) * conv_out).astype(jnp.bfloat16)
        key_out = (grad_in * value_part.astype(jnp.float32)).astype(jnp.bfloat16)
        value_out = (grad_in * key_part.astype(jnp.float32)).astype(jnp.bfloat16)
        return (running_sum + filter_terms, (query_out, key_out, value_out))
    start_sum = jnp.zeros((filter_count, seq_len), jnp.float32)
    running_sum, grads = lax.scan(one_group, start_sum, (regrouped(query_gate), regrouped(key_gate), regrouped(values), regrouped(out_grad)))
    query_grad = grads[0].reshape(channel_count, seq_len)
    key_grad = grads[1].reshape(channel_count, seq_len)
    value_grad = grads[2].reshape(channel_count, seq_len)
    filter_grad = running_sum * (1.0 / jnp.sqrt(jnp.float32(seq_len * group_count)))
    return (query_grad, key_grad, value_grad, filter_grad)
```

```python
import ml_dtypes
import numpy as np
import jax
import jax.numpy as jnp
from jax import lax
from jax.experimental import pallas as pl
from jax.experimental.pallas import tpu as pltpu
from jax.sharding import Mesh
from jax.sharding import PartitionSpec as P

N = 16384
ROWS = 72
F32 = jnp.float32
BF16 = jnp.bfloat16
MSG = 18


def split_table(table):
    high = table.astype(ml_dtypes.bfloat16)
    low = (table - high.astype(np.float64)).astype(ml_dtypes.bfloat16)
    return high, low


def tables():
    k1 = np.arange(ROWS)
    live = (k1 <= 64).astype(np.float64)
    t1 = np.arange(64)
    t2 = np.arange(128)
    turn = 2 * np.pi / 128

    angle = turn * (k1[:, None] * t1[None, :] % 128)
    first = np.concatenate([live[:, None] * np.cos(angle), -live[:, None] * np.sin(angle)])
    high, low = split_table(first)
    first3 = np.concatenate([high, high, low], axis=1)

    taps3 = []
    for parity in range(2):
        part = np.tile(first[:, parity::2], (1, 4))
        high, low = split_table(part)
        taps3 += [high, high, low]
    taps3 = np.concatenate(taps3, axis=1)

    angle = 2 * np.pi / N * (k1[:, None] * t2[None, :] % N)
    twist = np.stack([live[:, None] * np.cos(angle), live[:, None] * np.sin(angle)]).astype(np.float32)

    angle = turn * (t2[:, None] * t2[None, :] % 128)
    cos, sin = np.cos(angle), np.sin(angle)
    second = np.block([[cos, -sin], [sin, cos]])
    high, low = split_table(second)
    second3 = np.concatenate([high, low, high], axis=0)

    weight = live * np.where((k1 == 0) | (k1 == 64), 1.0, 2.0) / N
    angle = turn * (t1[:, None] * k1[None, :] % 128)
    last = np.concatenate([weight * np.cos(angle), weight * np.sin(angle)], axis=1)
    last3, lags3 = [], []
    for half in range(2):
        part = last[half * 32 : half * 32 + 32]
        high, low = split_table(part)
        last3.append(np.concatenate([high, high, low], axis=1))
        part = np.concatenate([np.tile(part[parity::2].T, (1, 8)) for parity in range(2)], axis=1)
        high, low = split_table(part)
        lags3.append(np.concatenate([high, low, high], axis=0))
    return first3, taps3, twist, second3, np.stack(last3), np.stack(lags3)


def halves(x):
    high = x.astype(BF16)
    return high, (x - high.astype(F32)).astype(BF16)


def lanes3(x):
    high, low = halves(x)
    return jnp.concatenate([high, low, high], axis=1)


def lanes3_table_last(x):
    high, low = halves(x)
    return jnp.concatenate([high, high, low], axis=1)


def rows3(x):
    high, low = halves(x)
    return jnp.concatenate([high, low, high], axis=0)


def mm(a, b):
    return jnp.dot(a, b, preferred_element_type=F32)


def turned(x_re, x_im, twist_ref):
    cos, sin = twist_ref[0], twist_ref[1]
    return x_re * cos + x_im * sin, x_im * cos - x_re * sin


def second_stage(stacked, second_ref):
    return mm(lanes3_table_last(stacked), second_ref[...])


def lane_group(width, rows):
    return lax.broadcasted_iota(jnp.int32, (rows, 128), 1) // width


def pack_kernel(q_ref, k_ref, v_ref, g_ref, f_ref, out_ref):
    gate_in = k_ref[...].astype(F32) * v_ref[...].astype(F32)
    grad_conv = g_ref[...].astype(F32) * q_ref[...].astype(F32)
    for copy in range(2):
        base = copy * 16 * MSG
        for j in range(8):
            cols = slice(j * 128, j * 128 + 128)
            out_ref[pl.ds(base + j, 16, stride=MSG), :] = gate_in[:, cols]
            out_ref[pl.ds(base + 8 + j, 16, stride=MSG), :] = grad_conv[:, cols]
    for high in range(2):
        taps = jnp.concatenate(
            [f_ref[(high * 8 + m) * 16 : (high * 8 + m) * 16 + 16, :] for m in range(8)], axis=1
        )
        for copy in range(2):
            out_ref[pl.ds(copy * 16 * MSG + 16 + high, 16, stride=MSG), :] = taps


def forward_kernel(half_ref, in_ref, first_ref, twist_ref, second_ref, lags_ref, spec_ref, out_ref, taps_t, lags_t):
    columns = []
    for array in range(2):
        for chan in range(4):
            tiles = [
                in_ref[(block * 4 + chan) * MSG + array * 8 : (block * 4 + chan) * MSG + array * 8 + 8, :]
                for block in range(8)
            ]
            columns.append(jnp.concatenate(tiles, axis=0))
    signals = jnp.concatenate(columns, axis=1)
    section = mm(first_ref[...], rows3(signals))
    stacked = []
    for s in range(8):
        cols = slice(s * 128, s * 128 + 128)
        re, im = turned(section[:ROWS, cols], section[ROWS:, cols], twist_ref)
        stacked.append(jnp.concatenate([re, im], axis=1))
    spec = second_stage(jnp.concatenate(stacked, axis=0), second_ref)
    spec_ref[...] = spec

    sum_re = jnp.zeros((ROWS, 128), F32)
    sum_im = jnp.zeros((ROWS, 128), F32)
    for chan in range(4):
        x = spec[chan * ROWS : chan * ROWS + ROWS]
        g = spec[(4 + chan) * ROWS : (4 + chan) * ROWS + ROWS]
        sum_re += g[:, :128] * x[:, :128] + g[:, 128:] * x[:, 128:]
        sum_im += g[:, :128] * x[:, 128:] - g[:, 128:] * x[:, :128]
    back = second_stage(jnp.concatenate([sum_re, sum_im], axis=1), second_ref)
    re, im = turned(back[:, :128], back[:, 128:], twist_ref)
    flipped = jnp.concatenate([re, im], axis=0).T
    lags = mm(lanes3_table_last(flipped), lags_ref[half_ref[0]]) * np.float32(1.0 / np.sqrt(32768.0))
    lags_t[:128, :] = lags[:, :128]
    lags_t[128:, :] = lags[:, 128:]

    group8 = lane_group(16, 8)
    group4 = lane_group(32, 8)
    zero = jnp.zeros((8, 128), F32)
    for high in range(2):
        taps = in_ref[pl.ds(16 + high, 32, stride=MSG), :]
        taps_t[...] = jnp.concatenate([taps] * 4, axis=0).T
        base = high * 64
        for b in range(4):
            row = zero
            for a in range(4):
                row = jnp.where(group4 == a, taps_t[pl.ds(4 * a + b, 8, stride=16), :], row)
            out_ref[pl.ds(base + b, 8, stride=8), :] = row
        for b in range(2):
            row = zero
            for a in range(8):
                row = jnp.where(group8 == a, lags_t[pl.ds(high * 128 + 2 * a + b, 8, stride=16), :], row)
            out_ref[pl.ds(base + 4 + b, 8, stride=8), :] = row
        for b in range(2):
            out_ref[pl.ds(base + 6 + b, 8, stride=8), :] = zero


def backward_kernel(half_ref, in_ref, spec_ref, taps_ref, twist_ref, second_ref, last_ref, out_ref, taps_t, lags_t):
    group8 = lane_group(16, 16)
    group4 = lane_group(32, 16)
    for b in range(4):
        row = in_ref[pl.ds(b, 16, stride=8), :]
        for a in range(4):
            taps_t[pl.ds(4 * a + b, 16, stride=16), :] = jnp.where(group4 == a, row, 0.0)
    for b in range(2):
        row = in_ref[pl.ds(4 + b, 16, stride=8), :]
        for a in range(8):
            lags_t[pl.ds(2 * a + b, 16, stride=16), :] = jnp.where(group8 == a, row, 0.0)
    for high in range(2):
        flipped = lags_t[high * 128 : high * 128 + 128, :].T
        total = flipped[:16]
        for a in range(1, 8):
            total += flipped[a * 16 : a * 16 + 16]
        out_ref[pl.ds(16 + high, 16, stride=MSG), :] = total

    taps = jnp.concatenate([lanes3(taps_t[:128, :]), lanes3(taps_t[128:, :])], axis=1)
    section = lax.dot_general(
        taps_ref[...], taps, (((1,), (1,)), ((), ())), preferred_element_type=F32
    )
    re, im = turned(section[:ROWS], section[ROWS:], twist_ref)
    filt = second_stage(jnp.concatenate([re, im], axis=1), second_ref)
    h_re, h_im = filt[:, :128], filt[:, 128:]

    products = []
    for s in range(8):
        re, im = spec_ref[s * ROWS : s * ROWS + ROWS, :128], spec_ref[s * ROWS : s * ROWS + ROWS, 128:]
        if s < 4:
            products.append(jnp.concatenate([re * h_re - im * h_im, -(re * h_im + im * h_re)], axis=1))
        else:
            products.append(jnp.concatenate([re * h_re + im * h_im, re * h_im - im * h_re], axis=1))
    back = second_stage(jnp.concatenate(products, axis=0), second_ref)
    columns = []
    for s in range(8):
        part = back[s * ROWS : s * ROWS + ROWS]
        re, im = turned(part[:, :128], part[:, 128:], twist_ref)
        columns.append(jnp.concatenate([re, im], axis=0))
    landed = mm(last_ref[half_ref[0]], rows3(jnp.concatenate(columns, axis=1)))
    for s in range(8):
        array, chan = s // 4, s % 4
        for block in range(4):
            start = (block * 4 + chan) * MSG + array * 8
            out_ref[start : start + 8, :] = landed[block * 8 : block * 8 + 8, s * 128 : s * 128 + 128]


def finish_kernel(in_ref, k_ref, v_ref, g_ref, q_out, k_out, v_out, f_out):
    for j in range(8):
        cols = slice(j * 128, j * 128 + 128)
        conv = in_ref[pl.ds(j, 16, stride=MSG), :]
        grad = in_ref[pl.ds(8 + j, 16, stride=MSG), :]
        q_out[:, cols] = (g_ref[:, cols].astype(F32) * conv).astype(BF16)
        k_out[:, cols] = (grad * v_ref[:, cols].astype(F32)).astype(BF16)
        v_out[:, cols] = (grad * k_ref[:, cols].astype(F32)).astype(BF16)
    for high in range(2):
        rows = in_ref[pl.ds(16 + high, 16, stride=MSG), :]
        for m in range(8):
            start = (high * 8 + m) * 16
            f_out[start : start + 16, :] = rows[:, m * 16 : m * 16 + 16]


SMEM = pl.BlockSpec(memory_space=pltpu.SMEM)
VMEM = pl.BlockSpec(memory_space=pltpu.VMEM)
PARAMS = pltpu.CompilerParams(vmem_limit_bytes=32 * 1024 * 1024)


def shape(*dims, dtype=F32):
    return jax.ShapeDtypeStruct(dims, dtype)


def on_device(q, k, v, filters, g):
    first3, taps3, twist, second3, last3, lags3 = (jnp.asarray(t) for t in tables())
    half = lax.axis_index("zh").astype(jnp.int32).reshape(1)

    packed = pl.pallas_call(
        pack_kernel, out_shape=shape(32 * MSG, 128), in_specs=[VMEM] * 5, out_specs=VMEM, compiler_params=PARAMS
    )(q, k, v, g, filters)
    arrived = lax.all_to_all(
        packed.reshape(32, MSG // 2, 2, 128), ("zh", "x", "zg"), split_axis=0, concat_axis=0, tiled=True
    ).reshape(32 * MSG, 128)

    spec, sent = pl.pallas_call(
        forward_kernel,
        out_shape=(shape(8 * ROWS, 256), shape(128, 128)),
        in_specs=[SMEM] + [VMEM] * 5,
        out_specs=(VMEM, VMEM),
        scratch_shapes=[pltpu.VMEM((128, 128), F32), pltpu.VMEM((256, 128), F32)],
        compiler_params=PARAMS,
    )(half, arrived, first3, twist, second3, lags3)
    swapped = lax.all_to_all(
        sent.reshape(16, 8, 128), ("zb", "y", "core"), split_axis=0, concat_axis=0, tiled=True
    ).reshape(128, 128)

    landed = pl.pallas_call(
        backward_kernel,
        out_shape=shape(16 * MSG, 128),
        in_specs=[SMEM] + [VMEM] * 6,
        out_specs=VMEM,
        scratch_shapes=[pltpu.VMEM((256, 128), F32), pltpu.VMEM((256, 128), F32)],
        compiler_params=PARAMS,
    )(half, swapped, spec, taps3, twist, second3, last3)
    home = lax.all_to_all(
        landed.reshape(16, MSG // 2, 2, 128), ("x", "zg"), split_axis=0, concat_axis=0, tiled=True
    ).reshape(16 * MSG, 128)

    out = shape(*q.shape, dtype=BF16)
    return pl.pallas_call(
        finish_kernel,
        out_shape=(out, out, out, shape(*filters.shape)),
        in_specs=[VMEM] * 4,
        out_specs=(VMEM,) * 4,
        compiler_params=PARAMS,
    )(home, k, v, g)


def solution(mesh):
    fine = Mesh(mesh.devices.reshape(2, 4, 4, 2, 4, 2), ("zh", "x", "zg", "zb", "y", "core"))
    seq, chan = ("zh", "x"), ("zg", "zb", "y", "core")
    gates, taps = P(chan, seq), P(None, seq + chan)
    return jax.shard_map(
        on_device,
        mesh=fine,
        in_specs=(gates, gates, gates, taps, gates),
        out_specs=(gates, gates, gates, taps),
        check_vma=False,
    )
```

```python
import ml_dtypes
import numpy as np
import jax
import jax.numpy as jnp
from jax import lax
from jax.experimental import pallas as pl
from jax.experimental.pallas import tpu as pltpu
from jax.sharding import Mesh
from jax.sharding import PartitionSpec as P

N = 16384
ROWS = 72
F32 = jnp.float32
BF16 = jnp.bfloat16
MSG = 18


def half_of(group, window):
    return window ^ (group // 2)


def split_table(table):
    high = table.astype(ml_dtypes.bfloat16)
    low = (table - high.astype(np.float64)).astype(ml_dtypes.bfloat16)
    return high, low


def tables():
    k1 = np.arange(ROWS)
    live = (k1 <= 64).astype(np.float64)
    t1 = np.arange(64)
    t2 = np.arange(128)
    turn = 2 * np.pi / 128

    angle = turn * (k1[:, None] * t1[None, :] % 128)
    first = np.concatenate([live[:, None] * np.cos(angle), -live[:, None] * np.sin(angle)])
    high, low = split_table(first)
    first3 = np.concatenate([high, high, low], axis=1)

    taps3 = []
    for parity in range(2):
        part = np.tile(first[:, parity::2], (1, 4))
        high, low = split_table(part)
        taps3 += [high, high, low]
    taps3 = np.concatenate(taps3, axis=1)

    angle = 2 * np.pi / N * (k1[:, None] * t2[None, :] % N)
    twist = np.stack([live[:, None] * np.cos(angle), live[:, None] * np.sin(angle)]).astype(np.float32)

    angle = turn * (t2[:, None] * t2[None, :] % 128)
    cos, sin = np.cos(angle), np.sin(angle)
    second = np.block([[cos, -sin], [sin, cos]])
    high, low = split_table(second)
    second3 = np.concatenate([high, low, high], axis=0)

    weight = live * np.where((k1 == 0) | (k1 == 64), 1.0, 2.0) / N
    angle = turn * (t1[:, None] * k1[None, :] % 128)
    last = np.concatenate([weight * np.cos(angle), weight * np.sin(angle)], axis=1)
    last3, lags3 = [], []
    for half in range(2):
        high, low = split_table(last[half * 32 : half * 32 + 32])
        last3.append(np.concatenate([high, high, low], axis=1))
    for window in range(2):
        rows = [half_of(group, window) * 32 + x * 8 + group * 2 for x in range(4) for group in range(4)]
        part = np.concatenate([np.tile(last[np.array(rows) + parity].T, (1, 8)) for parity in range(2)], axis=1)
        high, low = split_table(part)
        lags3.append(np.concatenate([high, low, high], axis=0))
    return first3, taps3, twist, second3, np.stack(last3), np.stack(lags3)


def halves(x):
    high = x.astype(BF16)
    return high, (x - high.astype(F32)).astype(BF16)


def lanes3(x):
    high, low = halves(x)
    return jnp.concatenate([high, low, high], axis=1)


def lanes3_table_last(x):
    high, low = halves(x)
    return jnp.concatenate([high, high, low], axis=1)


def rows3(x):
    high, low = halves(x)
    return jnp.concatenate([high, low, high], axis=0)


def mm(a, b):
    return jnp.dot(a, b, preferred_element_type=F32)


def turned(x_re, x_im, twist_ref):
    cos, sin = twist_ref[0], twist_ref[1]
    return x_re * cos + x_im * sin, x_im * cos - x_re * sin


def second_stage(stacked, second_ref):
    return mm(lanes3_table_last(stacked), second_ref[...])


def lane_group(width, rows):
    return lax.broadcasted_iota(jnp.int32, (rows, 128), 1) // width


def pack_kernel(q_hbm, k_hbm, v_hbm, g_hbm, f_hbm, out_ref, q_ref, k_ref, v_ref, g_ref, f_ref, sems):
    sources = (f_hbm, k_hbm, v_hbm, g_hbm, q_hbm)
    targets = (f_ref, k_ref, v_ref, g_ref, q_ref)
    copies = [pltpu.make_async_copy(source, target, sems.at[i]) for i, (source, target) in enumerate(zip(sources, targets))]
    for copy in copies:
        copy.start()
    for copy in copies:
        copy.wait()
    gate_in = k_ref[...].astype(F32) * v_ref[...].astype(F32)
    grad_conv = g_ref[...].astype(F32) * q_ref[...].astype(F32)
    for copy in range(2):
        base = copy * 16 * MSG
        for j in range(8):
            cols = slice(j * 128, j * 128 + 128)
            out_ref[pl.ds(base + j, 16, stride=MSG), :] = gate_in[:, cols]
            out_ref[pl.ds(base + 8 + j, 16, stride=MSG), :] = grad_conv[:, cols]
    for high in range(2):
        flipped = f_ref[:, high * 128 : high * 128 + 128].T
        taps = jnp.concatenate([flipped[m * 16 : m * 16 + 16, :] for m in range(8)], axis=1)
        for copy in range(2):
            out_ref[pl.ds(copy * 16 * MSG + 16 + high, 16, stride=MSG), :] = taps


def forward_kernel(window_ref, in_ref, first_ref, twist_ref, second_ref, lags_ref, spec_ref, out_ref, taps_t, lags_t):
    columns = []
    for array in range(2):
        for chan in range(4):
            tiles = [
                in_ref[(block * 4 + chan) * MSG + array * 8 : (block * 4 + chan) * MSG + array * 8 + 8, :]
                for block in range(8)
            ]
            columns.append(jnp.concatenate(tiles, axis=0))
    signals = jnp.concatenate(columns, axis=1)
    section = mm(first_ref[...], rows3(signals))
    stacked = []
    for s in range(8):
        cols = slice(s * 128, s * 128 + 128)
        re, im = turned(section[:ROWS, cols], section[ROWS:, cols], twist_ref)
        stacked.append(jnp.concatenate([re, im], axis=1))
    spec = second_stage(jnp.concatenate(stacked, axis=0), second_ref)
    spec_ref[...] = spec

    sum_re = jnp.zeros((ROWS, 128), F32)
    sum_im = jnp.zeros((ROWS, 128), F32)
    for chan in range(4):
        x = spec[chan * ROWS : chan * ROWS + ROWS]
        g = spec[(4 + chan) * ROWS : (4 + chan) * ROWS + ROWS]
        sum_re += g[:, :128] * x[:, :128] + g[:, 128:] * x[:, 128:]
        sum_im += g[:, :128] * x[:, 128:] - g[:, 128:] * x[:, :128]
    back = second_stage(jnp.concatenate([sum_re, sum_im], axis=1), second_ref)
    re, im = turned(back[:, :128], back[:, 128:], twist_ref)
    flipped = jnp.concatenate([re, im], axis=0).T
    lags = mm(lanes3_table_last(flipped), lags_ref[window_ref[0]]) * np.float32(1.0 / np.sqrt(32768.0))
    lags_t[:128, :] = lags[:, :128]
    lags_t[128:, :] = lags[:, 128:]

    group8 = lane_group(16, 8)
    group4 = lane_group(32, 8)
    zero = jnp.zeros((8, 128), F32)
    for high in range(2):
        taps = in_ref[pl.ds(16 + high, 32, stride=MSG), :]
        taps_t[...] = jnp.concatenate([taps] * 4, axis=0).T
        base = high * 64
        for b in range(4):
            row = zero
            for a in range(4):
                row = jnp.where(group4 == a, taps_t[pl.ds(4 * a + b, 8, stride=16), :], row)
            out_ref[pl.ds(base + b, 8, stride=8), :] = row
        for b in range(2):
            row = zero
            for a in range(8):
                row = jnp.where(group8 == a, lags_t[pl.ds(high * 128 + 2 * a + b, 8, stride=16), :], row)
            out_ref[pl.ds(base + 4 + b, 8, stride=8), :] = row
        for b in range(2):
            out_ref[pl.ds(base + 6 + b, 8, stride=8), :] = zero


def backward_kernel(window_ref, in_ref, spec_ref, taps_ref, twist_ref, second_ref, last_ref, out_ref, taps_t, lags_t):
    group8 = lane_group(16, 16)
    group4 = lane_group(32, 16)
    for b in range(4):
        row = in_ref[pl.ds(b, 16, stride=8), :]
        for a in range(4):
            taps_t[pl.ds(4 * a + b, 16, stride=16), :] = jnp.where(group4 == a, row, 0.0)
    for b in range(2):
        row = in_ref[pl.ds(4 + b, 16, stride=8), :]
        for a in range(8):
            lags_t[pl.ds(2 * a + b, 16, stride=16), :] = jnp.where(group8 == a, row, 0.0)
    for high in range(2):
        flipped = lags_t[high * 128 : high * 128 + 128, :].T
        total = flipped[:16]
        for a in range(1, 8):
            total += flipped[a * 16 : a * 16 + 16]
        out_ref[pl.ds(16 + high, 16, stride=MSG), :] = total

    taps = jnp.concatenate([lanes3(taps_t[:128, :]), lanes3(taps_t[128:, :])], axis=1)
    section = lax.dot_general(
        taps_ref[...], taps, (((1,), (1,)), ((), ())), preferred_element_type=F32
    )
    re, im = turned(section[:ROWS], section[ROWS:], twist_ref)
    filt = second_stage(jnp.concatenate([re, im], axis=1), second_ref)
    h_re, h_im = filt[:, :128], filt[:, 128:]

    products = []
    for s in range(8):
        re, im = spec_ref[s * ROWS : s * ROWS + ROWS, :128], spec_ref[s * ROWS : s * ROWS + ROWS, 128:]
        if s < 4:
            products.append(jnp.concatenate([re * h_re - im * h_im, -(re * h_im + im * h_re)], axis=1))
        else:
            products.append(jnp.concatenate([re * h_re + im * h_im, re * h_im - im * h_re], axis=1))
    back = second_stage(jnp.concatenate(products, axis=0), second_ref)
    columns = []
    for s in range(8):
        part = back[s * ROWS : s * ROWS + ROWS]
        re, im = turned(part[:, :128], part[:, 128:], twist_ref)
        columns.append(jnp.concatenate([re, im], axis=0))
    for pair in range(2):
        order = [array * 4 + pair * 2 + chan for array in range(2) for chan in range(2)]
        landed = mm(last_ref[window_ref[0] ^ pair], rows3(jnp.concatenate([columns[s] for s in order], axis=1)))
        for i, s in enumerate(order):
            array, chan = s // 4, s % 4
            for block in range(4):
                start = (block * 4 + chan) * MSG + array * 8
                out_ref[start : start + 8, :] = landed[block * 8 : block * 8 + 8, i * 128 : i * 128 + 128]


def finish_kernel(in_ref, k_ref, v_ref, g_ref, q_out, k_out, v_out, f_out):
    for j in range(8):
        cols = slice(j * 128, j * 128 + 128)
        conv = in_ref[pl.ds(j, 16, stride=MSG), :]
        grad = in_ref[pl.ds(8 + j, 16, stride=MSG), :]
        q_out[:, cols] = (g_ref[:, cols].astype(F32) * conv).astype(BF16)
        k_out[:, cols] = (grad * v_ref[:, cols].astype(F32)).astype(BF16)
        v_out[:, cols] = (grad * k_ref[:, cols].astype(F32)).astype(BF16)
    for high in range(2):
        flipped = in_ref[pl.ds(16 + high, 16, stride=MSG), :].T
        f_out[:, high * 128 : high * 128 + 128] = jnp.concatenate(
            [flipped[m * 16 : m * 16 + 16, :] for m in range(8)], axis=1
        )


SMEM = pl.BlockSpec(memory_space=pltpu.SMEM)
HBM = pl.BlockSpec(memory_space=pltpu.HBM)
VMEM = pl.BlockSpec(memory_space=pltpu.VMEM)
PARAMS = pltpu.CompilerParams(vmem_limit_bytes=32 * 1024 * 1024)


WINDOWS = [
    [half_of(group, window) * 16 + x * 4 + group for x in range(4) for group in range(4)] for window in range(2)
]


def shape(*dims, dtype=F32):
    return jax.ShapeDtypeStruct(dims, dtype)


def on_device(q, k, v, filters, g):
    first3, taps3, twist, second3, last3, lags3 = (jnp.asarray(t) for t in tables())
    window = (lax.axis_index("zh") ^ (lax.axis_index("zg") // 2)).astype(jnp.int32).reshape(1)

    packed = pl.pallas_call(
        pack_kernel,
        out_shape=shape(32 * MSG, 128),
        in_specs=[HBM] * 5,
        out_specs=VMEM,
        scratch_shapes=[pltpu.VMEM(q.shape, BF16)] * 4
        + [pltpu.VMEM(filters.shape[::-1], F32), pltpu.SemaphoreType.DMA((5,))],
        compiler_params=pltpu.CompilerParams(vmem_limit_bytes=60 * 1024 * 1024),
    )(q, k, v, g, filters.T)
    arrived = lax.all_to_all(
        packed.reshape(32, MSG // 2, 2, 128), ("zh", "x", "zg"), split_axis=0, concat_axis=0, tiled=True
    ).reshape(32 * MSG, 128)

    spec, sent = pl.pallas_call(
        forward_kernel,
        out_shape=(shape(8 * ROWS, 256), shape(128, 128)),
        in_specs=[SMEM] + [VMEM] * 5,
        out_specs=(VMEM, VMEM),
        scratch_shapes=[pltpu.VMEM((128, 128), F32), pltpu.VMEM((256, 128), F32)],
        compiler_params=PARAMS,
    )(window, arrived, first3, twist, second3, lags3)
    swapped = lax.all_to_all(
        sent.reshape(16, 8, 128), ("zb", "y", "core"), split_axis=0, concat_axis=0, tiled=True
    ).reshape(128, 128)

    landed = pl.pallas_call(
        backward_kernel,
        out_shape=shape(16 * MSG, 128),
        in_specs=[SMEM] + [VMEM] * 6,
        out_specs=VMEM,
        scratch_shapes=[pltpu.VMEM((256, 128), F32), pltpu.VMEM((256, 128), F32)],
        compiler_params=PARAMS,
    )(window, swapped, spec, taps3, twist, second3, last3)
    home = lax.all_to_all(
        landed.reshape(16, MSG // 2, 2, 128),
        ("zh", "x", "zg"),
        split_axis=0,
        concat_axis=0,
        axis_index_groups=WINDOWS,
        tiled=True,
    ).reshape(16 * MSG, 128)

    out = shape(*q.shape, dtype=BF16)
    q_grad, k_grad, v_grad, f_grad = pl.pallas_call(
        finish_kernel,
        out_shape=(out, out, out, shape(*filters.shape[::-1])),
        in_specs=[VMEM] * 4,
        out_specs=(VMEM,) * 4,
        compiler_params=PARAMS,
    )(home, k, v, g)
    return q_grad, k_grad, v_grad, f_grad.T


def solution(mesh):
    fine = Mesh(mesh.devices.reshape(2, 4, 4, 2, 4, 2), ("zh", "x", "zg", "zb", "y", "core"))
    seq, chan = ("zh", "x"), ("zg", "zb", "y", "core")
    gates, taps = P(chan, seq), P(None, seq + chan)
    return jax.shard_map(
        on_device,
        mesh=fine,
        in_specs=(gates, gates, gates, taps, gates),
        out_specs=(gates, gates, gates, taps),
        check_vma=False,
    )
```

```python
import ml_dtypes
import numpy as np
import jax
import jax.numpy as jnp
from jax import lax
from jax.experimental import pallas as pl
from jax.experimental.pallas import tpu as pltpu
from jax.sharding import Mesh
from jax.sharding import PartitionSpec as P

N = 16384
ROWS = 72
F32 = jnp.float32
BF16 = jnp.bfloat16
MSG = 18


def half_of(group, window):
    return window ^ (group // 2)


WORKERS = [(x, group) for x in range(4) for group in range(4) if (x, group) not in ((0, 3), (2, 1))]
WORKERS = [(0, 3)] + WORKERS[:7] + [(2, 1)] + WORKERS[7:]
ORDER = [(1, r) for r in range(8, 16)] + [(0, r) for r in range(16)] + [(1, r) for r in range(8)]


LEAD = 12


def source_slot(half, x, group):
    return ORDER.index((half, WORKERS.index((x, group))))


def device_of(half, worker):
    return half * 16 + worker[0] * 4 + worker[1]


def split_table(table):
    high = table.astype(ml_dtypes.bfloat16)
    low = (table - high.astype(np.float64)).astype(ml_dtypes.bfloat16)
    return high, low


def tables():
    k1 = np.arange(ROWS)
    live = (k1 <= 64).astype(np.float64)
    t1 = np.arange(64)
    t2 = np.arange(128)
    turn = 2 * np.pi / 128

    angle = turn * (k1[:, None] * t1[None, :] % 128)
    first = np.concatenate([live[:, None] * np.cos(angle), -live[:, None] * np.sin(angle)])
    high, low = split_table(first)
    first3 = np.concatenate([high, high, low], axis=1)

    taps3 = []
    sources = np.array([device_of(half, WORKERS[r]) for half, r in ORDER])
    for parity in range(2):
        part = np.tile(first[:, 2 * sources + parity], (1, 4))
        high, low = split_table(part)
        taps3 += [high, high, low]
    taps3 = np.concatenate(taps3, axis=1)

    angle = 2 * np.pi / N * (k1[:, None] * t2[None, :] % N)
    twist = np.stack([live[:, None] * np.cos(angle), live[:, None] * np.sin(angle)]).astype(np.float32)

    angle = turn * (t2[:, None] * t2[None, :] % 128)
    cos, sin = np.cos(angle), np.sin(angle)
    second = np.block([[cos, -sin], [sin, cos]])
    high, low = split_table(second)
    second3 = np.concatenate([high, low, high], axis=0)

    weight = live * np.where((k1 == 0) | (k1 == 64), 1.0, 2.0) / N
    angle = turn * (t1[:, None] * k1[None, :] % 128)
    last = np.concatenate([weight * np.cos(angle), weight * np.sin(angle)], axis=1)
    last3, lags3 = [], []
    for half in range(2):
        high, low = split_table(last[half * 32 : half * 32 + 32])
        last3.append(np.concatenate([high, high, low], axis=1))
    for window in range(2):
        rows = [half_of(group, window) * 32 + x * 8 + group * 2 for x, group in WORKERS]
        part = np.concatenate([np.tile(last[np.array(rows) + parity].T, (1, 8)) for parity in range(2)], axis=1)
        high, low = split_table(part)
        lags3.append(np.concatenate([high, low, high], axis=0))
    return first3, taps3, twist, second3, np.stack(last3), np.stack(lags3)


def halves(x):
    high = x.astype(BF16)
    return high, (x - high.astype(F32)).astype(BF16)


def lanes3(x):
    high, low = halves(x)
    return jnp.concatenate([high, low, high], axis=1)


def lanes3_table_last(x):
    high, low = halves(x)
    return jnp.concatenate([high, high, low], axis=1)


def rows3(x):
    high, low = halves(x)
    return jnp.concatenate([high, low, high], axis=0)


def mm(a, b):
    return jnp.dot(a, b, preferred_element_type=F32)


def turned(x_re, x_im, twist_ref):
    cos, sin = twist_ref[0], twist_ref[1]
    return x_re * cos + x_im * sin, x_im * cos - x_re * sin


def second_stage(stacked, second_ref):
    return mm(lanes3_table_last(stacked), second_ref[...])


def lane_group(width, rows):
    return lax.broadcasted_iota(jnp.int32, (rows, 128), 1) // width


def put_messages(out_ref, row, values):
    out_ref[pl.ds(8 * MSG + row, 16, stride=MSG), :] = values
    out_ref[pl.ds(row, 8, stride=MSG), :] = values[8:]
    out_ref[pl.ds(24 * MSG + row, 8, stride=MSG), :] = values[:8]


def put_places(out_ref, start, values):
    out_ref[pl.ds(start, 4, stride=8), :] = values[4:]
    out_ref[pl.ds(start + 32, 4, stride=8), :] = values[:4]


def get_places(in_ref, row):
    return jnp.concatenate(
        [in_ref[pl.ds((m ^ LEAD) * 8 + row, 4, stride=8), :] for m in range(0, 16, 4)], axis=0
    )


def pack_kernel(window_ref, q_hbm, k_hbm, v_hbm, g_hbm, f_hbm, out_ref, q_ref, k_ref, v_ref, g_ref, f_ref, sems):
    sources = (f_hbm, k_hbm, v_hbm, g_hbm, q_hbm)
    targets = (f_ref, k_ref, v_ref, g_ref, q_ref)
    copies = [pltpu.make_async_copy(source, target, sems.at[i]) for i, (source, target) in enumerate(zip(sources, targets))]
    for copy in copies:
        copy.start()
    for copy in copies:
        copy.wait()
    gate_in = k_ref[...].astype(F32) * v_ref[...].astype(F32)
    grad_conv = g_ref[...].astype(F32) * q_ref[...].astype(F32)
    for j in range(8):
        cols = slice(j * 128, j * 128 + 128)
        put_messages(out_ref, j, gate_in[:, cols])
        put_messages(out_ref, 8 + j, grad_conv[:, cols])
    for high in range(2):
        flipped = f_ref[:, high * 128 : high * 128 + 128].T
        taps = jnp.concatenate([flipped[m * 16 : m * 16 + 16, :] for m in range(8)], axis=1)
        put_messages(out_ref, 16 + high, taps)


def forward_kernel(window_ref, in_ref, first_ref, twist_ref, second_ref, lags_ref, spec_ref, out_ref, taps_t, lags_t):
    columns = []
    for array in range(2):
        for chan in range(4):
            starts = [source_slot(block // 4, block % 4, chan) * MSG + array * 8 for block in range(8)]
            columns.append(jnp.concatenate([in_ref[start : start + 8, :] for start in starts], axis=0))
    signals = jnp.concatenate(columns, axis=1)
    section = mm(first_ref[...], rows3(signals))
    stacked = []
    for s in range(8):
        cols = slice(s * 128, s * 128 + 128)
        re, im = turned(section[:ROWS, cols], section[ROWS:, cols], twist_ref)
        stacked.append(jnp.concatenate([re, im], axis=1))
    spec = second_stage(jnp.concatenate(stacked, axis=0), second_ref)
    spec_ref[...] = spec

    sum_re = jnp.zeros((ROWS, 128), F32)
    sum_im = jnp.zeros((ROWS, 128), F32)
    for chan in range(4):
        x = spec[chan * ROWS : chan * ROWS + ROWS]
        g = spec[(4 + chan) * ROWS : (4 + chan) * ROWS + ROWS]
        sum_re += g[:, :128] * x[:, :128] + g[:, 128:] * x[:, 128:]
        sum_im += g[:, :128] * x[:, 128:] - g[:, 128:] * x[:, :128]
    back = second_stage(jnp.concatenate([sum_re, sum_im], axis=1), second_ref)
    re, im = turned(back[:, :128], back[:, 128:], twist_ref)
    flipped = jnp.concatenate([re, im], axis=0).T
    lags = mm(lanes3_table_last(flipped), lags_ref[window_ref[0]]) * np.float32(1.0 / np.sqrt(32768.0))
    lags_t[:128, :] = lags[:, :128]
    lags_t[128:, :] = lags[:, 128:]

    group8 = lane_group(16, 8)
    group4 = lane_group(32, 8)
    zero = jnp.zeros((8, 128), F32)
    for high in range(2):
        taps = in_ref[pl.ds(16 + high, 32, stride=MSG), :]
        taps_t[...] = jnp.concatenate([taps] * 4, axis=0).T
        base = (high ^ LEAD // 8) * 64
        for b in range(4):
            row = zero
            for a in range(4):
                row = jnp.where(group4 == a, taps_t[pl.ds(4 * a + b, 8, stride=16), :], row)
            put_places(out_ref, base + b, row)
        for b in range(2):
            row = zero
            for a in range(8):
                row = jnp.where(group8 == a, lags_t[pl.ds(high * 128 + 2 * a + b, 8, stride=16), :], row)
            put_places(out_ref, base + 4 + b, row)
        for b in range(2):
            out_ref[pl.ds(base + 6 + b, 8, stride=8), :] = zero


def backward_kernel(window_ref, in_ref, spec_ref, taps_ref, twist_ref, second_ref, last_ref, out_ref, taps_t, lags_t):
    group8 = lane_group(16, 16)
    group4 = lane_group(32, 16)
    for b in range(4):
        row = get_places(in_ref, b)
        for a in range(4):
            taps_t[pl.ds(4 * a + b, 16, stride=16), :] = jnp.where(group4 == a, row, 0.0)
    for b in range(2):
        row = get_places(in_ref, 4 + b)
        for a in range(8):
            lags_t[pl.ds(2 * a + b, 16, stride=16), :] = jnp.where(group8 == a, row, 0.0)
    for high in range(2):
        flipped = lags_t[high * 128 : high * 128 + 128, :].T
        total = flipped[:16]
        for a in range(1, 8):
            total += flipped[a * 16 : a * 16 + 16]
        out_ref[pl.ds(16 + high, 16, stride=MSG), :] = total

    taps = jnp.concatenate([lanes3(taps_t[:128, :]), lanes3(taps_t[128:, :])], axis=1)
    section = lax.dot_general(
        taps_ref[...], taps, (((1,), (1,)), ((), ())), preferred_element_type=F32
    )
    re, im = turned(section[:ROWS], section[ROWS:], twist_ref)
    filt = second_stage(jnp.concatenate([re, im], axis=1), second_ref)
    h_re, h_im = filt[:, :128], filt[:, 128:]

    products = []
    for s in range(8):
        re, im = spec_ref[s * ROWS : s * ROWS + ROWS, :128], spec_ref[s * ROWS : s * ROWS + ROWS, 128:]
        if s < 4:
            products.append(jnp.concatenate([re * h_re - im * h_im, -(re * h_im + im * h_re)], axis=1))
        else:
            products.append(jnp.concatenate([re * h_re + im * h_im, re * h_im - im * h_re], axis=1))
    back = second_stage(jnp.concatenate(products, axis=0), second_ref)
    columns = []
    for s in range(8):
        part = back[s * ROWS : s * ROWS + ROWS]
        re, im = turned(part[:, :128], part[:, 128:], twist_ref)
        columns.append(jnp.concatenate([re, im], axis=0))
    for pair in range(2):
        order = [array * 4 + pair * 2 + chan for array in range(2) for chan in range(2)]
        landed = mm(last_ref[window_ref[0] ^ pair], rows3(jnp.concatenate([columns[s] for s in order], axis=1)))
        for i, s in enumerate(order):
            array, chan = s // 4, s % 4
            for block in range(4):
                start = WORKERS.index((block, chan)) * MSG + array * 8
                out_ref[start : start + 8, :] = landed[block * 8 : block * 8 + 8, i * 128 : i * 128 + 128]


def finish_kernel(in_ref, k_ref, v_ref, g_ref, q_out, k_out, v_out, f_out):
    for j in range(8):
        cols = slice(j * 128, j * 128 + 128)
        conv = in_ref[pl.ds(j, 16, stride=MSG), :]
        grad = in_ref[pl.ds(8 + j, 16, stride=MSG), :]
        q_out[:, cols] = (g_ref[:, cols].astype(F32) * conv).astype(BF16)
        k_out[:, cols] = (grad * v_ref[:, cols].astype(F32)).astype(BF16)
        v_out[:, cols] = (grad * k_ref[:, cols].astype(F32)).astype(BF16)
    for high in range(2):
        flipped = in_ref[pl.ds(16 + high, 16, stride=MSG), :].T
        f_out[:, high * 128 : high * 128 + 128] = jnp.concatenate(
            [flipped[m * 16 : m * 16 + 16, :] for m in range(8)], axis=1
        )


SMEM = pl.BlockSpec(memory_space=pltpu.SMEM)
HBM = pl.BlockSpec(memory_space=pltpu.HBM)
VMEM = pl.BlockSpec(memory_space=pltpu.VMEM)
PARAMS = pltpu.CompilerParams(vmem_limit_bytes=32 * 1024 * 1024)


WINDOWS = [[device_of(half_of(worker[1], window), worker) for worker in WORKERS] for window in range(2)]


def shape(*dims, dtype=F32):
    return jax.ShapeDtypeStruct(dims, dtype)


def on_device(q, k, v, filters, g):
    first3, taps3, twist, second3, last3, lags3 = (jnp.asarray(t) for t in tables())
    window = (lax.axis_index("zh") ^ (lax.axis_index("zg") // 2)).astype(jnp.int32).reshape(1)

    packed = pl.pallas_call(
        pack_kernel,
        out_shape=shape(32 * MSG, 128),
        in_specs=[SMEM] + [HBM] * 5,
        out_specs=VMEM,
        scratch_shapes=[pltpu.VMEM(q.shape, BF16)] * 4
        + [pltpu.VMEM(filters.shape[::-1], F32), pltpu.SemaphoreType.DMA((5,))],
        compiler_params=pltpu.CompilerParams(vmem_limit_bytes=60 * 1024 * 1024),
    )(window, q, k, v, g, filters.T)
    arrived = lax.all_to_all(
        packed.reshape(32, MSG // 2, 2, 128),
        ("zh", "x", "zg"),
        split_axis=0,
        concat_axis=0,
        axis_index_groups=[[device_of(half, WORKERS[r]) for half, r in ORDER]],
        tiled=True,
    ).reshape(32 * MSG, 128)

    spec, sent = pl.pallas_call(
        forward_kernel,
        out_shape=(shape(8 * ROWS, 256), shape(128, 128)),
        in_specs=[SMEM] + [VMEM] * 5,
        out_specs=(VMEM, VMEM),
        scratch_shapes=[pltpu.VMEM((128, 128), F32), pltpu.VMEM((256, 128), F32)],
        compiler_params=PARAMS,
    )(window, arrived, first3, twist, second3, lags3)
    swapped = lax.all_to_all(
        sent.reshape(16, 8, 128),
        ("zb", "y", "core"),
        split_axis=0,
        concat_axis=0,
        axis_index_groups=[[slot ^ LEAD for slot in range(16)]],
        tiled=True,
    ).reshape(128, 128)

    landed = pl.pallas_call(
        backward_kernel,
        out_shape=shape(16 * MSG, 128),
        in_specs=[SMEM] + [VMEM] * 6,
        out_specs=VMEM,
        scratch_shapes=[pltpu.VMEM((256, 128), F32), pltpu.VMEM((256, 128), F32)],
        compiler_params=PARAMS,
    )(window, swapped, spec, taps3, twist, second3, last3)
    home = lax.all_to_all(
        landed.reshape(16, MSG // 2, 2, 128),
        ("zh", "x", "zg"),
        split_axis=0,
        concat_axis=0,
        axis_index_groups=WINDOWS,
        tiled=True,
    ).reshape(16 * MSG, 128)

    out = shape(*q.shape, dtype=BF16)
    q_grad, k_grad, v_grad, f_grad = pl.pallas_call(
        finish_kernel,
        out_shape=(out, out, out, shape(*filters.shape[::-1])),
        in_specs=[VMEM] * 4,
        out_specs=(VMEM,) * 4,
        compiler_params=PARAMS,
    )(home, k, v, g)
    return q_grad, k_grad, v_grad, f_grad.T


def solution(mesh):
    fine = Mesh(mesh.devices.reshape(2, 4, 4, 2, 4, 2), ("zh", "x", "zg", "zb", "y", "core"))
    seq, chan = ("zh", "x"), ("zg", "zb", "y", "core")
    gates, taps = P(chan, seq), P(None, seq + chan)
    return jax.shard_map(
        on_device,
        mesh=fine,
        in_specs=(gates, gates, gates, taps, gates),
        out_specs=(gates, gates, gates, taps),
        check_vma=False,
    )
```

```python
import ml_dtypes
import numpy as np
import jax
import jax.numpy as jnp
from jax import lax
from jax.experimental import pallas as pl
from jax.experimental.pallas import tpu as pltpu
from jax.sharding import Mesh
from jax.sharding import PartitionSpec as P

N = 16384
ROWS = 72
F32 = jnp.float32
BF16 = jnp.bfloat16
MSG = 18


def half_of(group, window):
    return window ^ (group // 2)


WORKERS = [(x, group) for x in range(4) for group in range(4) if (x, group) not in ((0, 3), (2, 1))]
WORKERS = [(0, 3)] + WORKERS[:7] + [(2, 1)] + WORKERS[7:]
ORDER = [(1, r) for r in range(8, 16)] + [(0, r) for r in range(16)] + [(1, r) for r in range(8)]


LEAD = 12


def source_slot(half, x, group):
    return ORDER.index((half, WORKERS.index((x, group))))


def device_of(half, worker):
    return half * 16 + worker[0] * 4 + worker[1]


def split_table(table):
    high = table.astype(ml_dtypes.bfloat16)
    low = (table - high.astype(np.float64)).astype(ml_dtypes.bfloat16)
    return high, low


def tables():
    k1 = np.arange(ROWS)
    live = (k1 <= 64).astype(np.float64)
    t1 = np.arange(64)
    t2 = np.arange(128)
    turn = 2 * np.pi / 128

    angle = turn * (k1[:, None] * t1[None, :] % 128)
    first = np.concatenate([live[:, None] * np.cos(angle), -live[:, None] * np.sin(angle)])
    high, low = split_table(first)
    first3 = np.concatenate([high, high, low], axis=1)

    taps3 = []
    sources = np.array([device_of(half, WORKERS[r]) for half, r in ORDER])
    for parity in range(2):
        part = np.tile(first[:, 2 * sources + parity], (1, 4))
        high, low = split_table(part)
        taps3 += [high, high, low]
    taps3 = np.concatenate(taps3, axis=1)

    angle = 2 * np.pi / N * (k1[:, None] * t2[None, :] % N)
    twist = np.stack([live[:, None] * np.cos(angle), live[:, None] * np.sin(angle)]).astype(np.float32)

    angle = turn * (t2[:, None] * t2[None, :] % 128)
    cos, sin = np.cos(angle), np.sin(angle)
    second = np.block([[cos, -sin], [sin, cos]])
    high, low = split_table(second)
    second3 = np.concatenate([high, low, high], axis=0)

    weight = live * np.where((k1 == 0) | (k1 == 64), 1.0, 2.0) / N
    angle = turn * (t1[:, None] * k1[None, :] % 128)
    last = np.concatenate([weight * np.cos(angle), weight * np.sin(angle)], axis=1)
    last3, lags3 = [], []
    for half in range(2):
        high, low = split_table(last[half * 32 : half * 32 + 32])
        last3.append(np.concatenate([high, high, low], axis=1))
    for window in range(2):
        rows = [half_of(group, window) * 32 + x * 8 + group * 2 for x, group in WORKERS]
        part = np.concatenate([np.tile(last[np.array(rows) + parity].T, (1, 8)) for parity in range(2)], axis=1)
        high, low = split_table(part)
        lags3.append(np.concatenate([high, low, high], axis=0))
    return first3, taps3, twist, second3, np.stack(last3), np.stack(lags3)


def halves(x):
    high = x.astype(BF16)
    return high, (x - high.astype(F32)).astype(BF16)


def lanes3(x):
    high, low = halves(x)
    return jnp.concatenate([high, low, high], axis=1)


def lanes3_table_last(x):
    high, low = halves(x)
    return jnp.concatenate([high, high, low], axis=1)


def rows3(x):
    high, low = halves(x)
    return jnp.concatenate([high, low, high], axis=0)


def mm(a, b):
    return jnp.dot(a, b, preferred_element_type=F32)


def turned(x_re, x_im, twist_ref):
    cos, sin = twist_ref[0], twist_ref[1]
    return x_re * cos + x_im * sin, x_im * cos - x_re * sin


def second_stage(stacked, second_ref):
    return mm(lanes3_table_last(stacked), second_ref[...])


def lane_group(width, rows):
    return lax.broadcasted_iota(jnp.int32, (rows, 128), 1) // width


def put_messages(out_ref, row, values):
    out_ref[pl.ds(8 * MSG + row, 16, stride=MSG), :] = values
    out_ref[pl.ds(row, 8, stride=MSG), :] = values[8:]
    out_ref[pl.ds(24 * MSG + row, 8, stride=MSG), :] = values[:8]


def put_places(out_ref, start, values):
    out_ref[pl.ds(start, 4, stride=8), :] = values[4:]
    out_ref[pl.ds(start + 32, 4, stride=8), :] = values[:4]


def get_places(in_ref, row):
    return jnp.concatenate(
        [in_ref[pl.ds((m ^ LEAD) * 8 + row, 4, stride=8), :] for m in range(0, 16, 4)], axis=0
    )


def pack_kernel(place_ref, q_ref, k_ref, v_ref, g_ref, f_ref, out_ref):
    gate_in = k_ref[...].astype(F32) * v_ref[...].astype(F32)
    grad_conv = g_ref[...].astype(F32) * q_ref[...].astype(F32)
    for j in range(8):
        cols = slice(j * 128, j * 128 + 128)
        put_messages(out_ref, j, gate_in[:, cols])
        put_messages(out_ref, 8 + j, grad_conv[:, cols])
    for high in range(2):
        flipped = f_ref[:, high * 128 : high * 128 + 128].T
        taps = jnp.concatenate([flipped[m * 16 : m * 16 + 16, :] for m in range(8)], axis=1)
        put_messages(out_ref, 16 + high, taps)


def forward_kernel(window_ref, in_ref, first_ref, twist_ref, second_ref, lags_ref, spec_ref, out_ref, taps_t, lags_t):
    columns = []
    for array in range(2):
        for chan in range(4):
            starts = [source_slot(block // 4, block % 4, chan) * MSG + array * 8 for block in range(8)]
            columns.append(jnp.concatenate([in_ref[start : start + 8, :] for start in starts], axis=0))
    signals = jnp.concatenate(columns, axis=1)
    section = mm(first_ref[...], rows3(signals))
    stacked = []
    for s in range(8):
        cols = slice(s * 128, s * 128 + 128)
        re, im = turned(section[:ROWS, cols], section[ROWS:, cols], twist_ref)
        stacked.append(jnp.concatenate([re, im], axis=1))
    spec = second_stage(jnp.concatenate(stacked, axis=0), second_ref)
    spec_ref[...] = spec

    sum_re = jnp.zeros((ROWS, 128), F32)
    sum_im = jnp.zeros((ROWS, 128), F32)
    for chan in range(4):
        x = spec[chan * ROWS : chan * ROWS + ROWS]
        g = spec[(4 + chan) * ROWS : (4 + chan) * ROWS + ROWS]
        sum_re += g[:, :128] * x[:, :128] + g[:, 128:] * x[:, 128:]
        sum_im += g[:, :128] * x[:, 128:] - g[:, 128:] * x[:, :128]
    back = second_stage(jnp.concatenate([sum_re, sum_im], axis=1), second_ref)
    re, im = turned(back[:, :128], back[:, 128:], twist_ref)
    flipped = jnp.concatenate([re, im], axis=0).T
    lags = mm(lanes3_table_last(flipped), lags_ref[window_ref[0]]) * np.float32(1.0 / np.sqrt(32768.0))
    lags_t[:128, :] = lags[:, :128]
    lags_t[128:, :] = lags[:, 128:]

    group8 = lane_group(16, 8)
    group4 = lane_group(32, 8)
    zero = jnp.zeros((8, 128), F32)
    for high in range(2):
        taps = in_ref[pl.ds(16 + high, 32, stride=MSG), :]
        taps_t[...] = jnp.concatenate([taps] * 4, axis=0).T
        base = (high ^ LEAD // 8) * 64
        for b in range(4):
            row = zero
            for a in range(4):
                row = jnp.where(group4 == a, taps_t[pl.ds(4 * a + b, 8, stride=16), :], row)
            put_places(out_ref, base + b, row)
        for b in range(2):
            row = zero
            for a in range(8):
                row = jnp.where(group8 == a, lags_t[pl.ds(high * 128 + 2 * a + b, 8, stride=16), :], row)
            put_places(out_ref, base + 4 + b, row)
        for b in range(2):
            out_ref[pl.ds(base + 6 + b, 8, stride=8), :] = zero


def backward_kernel(window_ref, in_ref, spec_ref, taps_ref, twist_ref, second_ref, last_ref, out_ref, taps_t, lags_t):
    group8 = lane_group(16, 16)
    group4 = lane_group(32, 16)
    for b in range(4):
        row = get_places(in_ref, b)
        for a in range(4):
            taps_t[pl.ds(4 * a + b, 16, stride=16), :] = jnp.where(group4 == a, row, 0.0)
    for b in range(2):
        row = get_places(in_ref, 4 + b)
        for a in range(8):
            lags_t[pl.ds(2 * a + b, 16, stride=16), :] = jnp.where(group8 == a, row, 0.0)
    for high in range(2):
        flipped = lags_t[high * 128 : high * 128 + 128, :].T
        total = flipped[:16]
        for a in range(1, 8):
            total += flipped[a * 16 : a * 16 + 16]
        out_ref[pl.ds(16 + high, 16, stride=MSG), :] = total

    taps = jnp.concatenate([lanes3(taps_t[:128, :]), lanes3(taps_t[128:, :])], axis=1)
    section = lax.dot_general(
        taps_ref[...], taps, (((1,), (1,)), ((), ())), preferred_element_type=F32
    )
    re, im = turned(section[:ROWS], section[ROWS:], twist_ref)
    filt = second_stage(jnp.concatenate([re, im], axis=1), second_ref)
    h_re, h_im = filt[:, :128], filt[:, 128:]

    products = []
    for s in range(8):
        re, im = spec_ref[s * ROWS : s * ROWS + ROWS, :128], spec_ref[s * ROWS : s * ROWS + ROWS, 128:]
        if s < 4:
            products.append(jnp.concatenate([re * h_re - im * h_im, -(re * h_im + im * h_re)], axis=1))
        else:
            products.append(jnp.concatenate([re * h_re + im * h_im, re * h_im - im * h_re], axis=1))
    back = second_stage(jnp.concatenate(products, axis=0), second_ref)
    columns = []
    for s in range(8):
        part = back[s * ROWS : s * ROWS + ROWS]
        re, im = turned(part[:, :128], part[:, 128:], twist_ref)
        columns.append(jnp.concatenate([re, im], axis=0))
    for pair in range(2):
        order = [array * 4 + pair * 2 + chan for array in range(2) for chan in range(2)]
        landed = mm(last_ref[window_ref[0] ^ pair], rows3(jnp.concatenate([columns[s] for s in order], axis=1)))
        for i, s in enumerate(order):
            array, chan = s // 4, s % 4
            for block in range(4):
                start = WORKERS.index((block, chan)) * MSG + array * 8
                out_ref[start : start + 8, :] = landed[block * 8 : block * 8 + 8, i * 128 : i * 128 + 128]


def finish_kernel(in_ref, k_ref, v_ref, g_ref, q_out, k_out, v_out, f_out):
    for j in range(8):
        cols = slice(j * 128, j * 128 + 128)
        conv = in_ref[pl.ds(j, 16, stride=MSG), :]
        grad = in_ref[pl.ds(8 + j, 16, stride=MSG), :]
        q_out[:, cols] = (g_ref[:, cols].astype(F32) * conv).astype(BF16)
        k_out[:, cols] = (grad * v_ref[:, cols].astype(F32)).astype(BF16)
        v_out[:, cols] = (grad * k_ref[:, cols].astype(F32)).astype(BF16)
    for high in range(2):
        flipped = in_ref[pl.ds(16 + high, 16, stride=MSG), :].T
        f_out[:, high * 128 : high * 128 + 128] = jnp.concatenate(
            [flipped[m * 16 : m * 16 + 16, :] for m in range(8)], axis=1
        )


SMEM = pl.BlockSpec(memory_space=pltpu.SMEM)
VMEM = pl.BlockSpec(memory_space=pltpu.VMEM)
PARAMS = pltpu.CompilerParams(vmem_limit_bytes=32 * 1024 * 1024)


WINDOWS = [[device_of(half_of(worker[1], window), worker) for worker in WORKERS] for window in range(2)]


def shape(*dims, dtype=F32):
    return jax.ShapeDtypeStruct(dims, dtype)


def on_device(q, k, v, filters, g):
    first3, taps3, twist, second3, last3, lags3 = (jnp.asarray(t) for t in tables())
    window = (lax.axis_index("zh") ^ (lax.axis_index("zg") // 2)).astype(jnp.int32).reshape(1)

    place = jnp.broadcast_to(window.astype(F32), (512, 128))
    packed = pl.pallas_call(
        pack_kernel,
        out_shape=shape(32 * MSG, 128),
        in_specs=[VMEM] * 6,
        out_specs=VMEM,
        compiler_params=PARAMS,
    )(place, q, k, v, g, filters.T)
    arrived = lax.all_to_all(
        packed.reshape(32, MSG // 2, 2, 128),
        ("zh", "x", "zg"),
        split_axis=0,
        concat_axis=0,
        axis_index_groups=[[device_of(half, WORKERS[r]) for half, r in ORDER]],
        tiled=True,
    ).reshape(32 * MSG, 128)

    spec, sent = pl.pallas_call(
        forward_kernel,
        out_shape=(shape(8 * ROWS, 256), shape(128, 128)),
        in_specs=[VMEM] * 6,
        out_specs=(VMEM, VMEM),
        scratch_shapes=[pltpu.VMEM((128, 128), F32), pltpu.VMEM((256, 128), F32)],
        compiler_params=PARAMS,
    )(window, arrived, first3, twist, second3, lags3)
    swapped = lax.all_to_all(
        sent.reshape(16, 8, 128),
        ("zb", "y", "core"),
        split_axis=0,
        concat_axis=0,
        axis_index_groups=[[slot ^ LEAD for slot in range(16)]],
        tiled=True,
    ).reshape(128, 128)

    landed = pl.pallas_call(
        backward_kernel,
        out_shape=shape(16 * MSG, 128),
        in_specs=[SMEM] + [VMEM] * 6,
        out_specs=VMEM,
        scratch_shapes=[pltpu.VMEM((256, 128), F32), pltpu.VMEM((256, 128), F32)],
        compiler_params=PARAMS,
    )(window, swapped, spec, taps3, twist, second3, last3)
    home = lax.all_to_all(
        landed.reshape(16, MSG // 2, 2, 128),
        ("zh", "x", "zg"),
        split_axis=0,
        concat_axis=0,
        axis_index_groups=WINDOWS,
        tiled=True,
    ).reshape(16 * MSG, 128)

    out = shape(*q.shape, dtype=BF16)
    q_grad, k_grad, v_grad, f_grad = pl.pallas_call(
        finish_kernel,
        out_shape=(out, out, out, shape(*filters.shape[::-1])),
        in_specs=[VMEM] * 4,
        out_specs=(VMEM,) * 4,
        compiler_params=PARAMS,
    )(home, k, v, g)
    return q_grad, k_grad, v_grad, f_grad.T


def solution(mesh):
    fine = Mesh(mesh.devices.reshape(2, 4, 4, 2, 4, 2), ("zh", "x", "zg", "zb", "y", "core"))
    seq, chan = ("zh", "x"), ("zg", "zb", "y", "core")
    gates, taps = P(chan, seq), P(None, seq + chan)
    return jax.shard_map(
        on_device,
        mesh=fine,
        in_specs=(gates, gates, gates, taps, gates),
        out_specs=(gates, gates, gates, taps),
        check_vma=False,
    )
```

```python
import ml_dtypes
import numpy as np
import jax
import jax.numpy as jnp
from jax import lax
from jax.experimental import pallas as pl
from jax.experimental.pallas import tpu as pltpu
from jax.sharding import Mesh
from jax.sharding import PartitionSpec as P

N = 16384
ROWS = 72
F32 = jnp.float32
BF16 = jnp.bfloat16
MSG = 18


LEAD = 12
LEAD_PLACE = 12


def split_table(table):
    high = table.astype(ml_dtypes.bfloat16)
    low = (table - high.astype(np.float64)).astype(ml_dtypes.bfloat16)
    return high, low


def tables():
    k1 = np.arange(ROWS)
    live = (k1 <= 64).astype(np.float64)
    t1 = np.arange(64)
    t2 = np.arange(128)
    turn = 2 * np.pi / 128

    angle = turn * (k1[:, None] * t1[None, :] % 128)
    first = np.concatenate([live[:, None] * np.cos(angle), -live[:, None] * np.sin(angle)])
    high, low = split_table(first)
    first3 = np.concatenate([high, high, low], axis=1)

    sources = np.arange(16) ^ LEAD
    taps3 = []
    for part in range(4):
        high, low = split_table(np.tile(first[:, 4 * sources + part], (1, 8)))
        taps3 += [high, high, low]
    taps3 = np.concatenate(taps3, axis=1)

    angle = 2 * np.pi / N * (k1[:, None] * t2[None, :] % N)
    twist = np.stack([live[:, None] * np.cos(angle), live[:, None] * np.sin(angle)]).astype(np.float32)

    angle = turn * (t2[:, None] * t2[None, :] % 128)
    cos, sin = np.cos(angle), np.sin(angle)
    second = np.block([[cos, -sin], [sin, cos]])
    high, low = split_table(second)
    second3 = np.concatenate([high, low, high], axis=0)

    weight = live * np.where((k1 == 0) | (k1 == 64), 1.0, 2.0) / N
    angle = turn * (t1[:, None] * k1[None, :] % 128)
    last = np.concatenate([weight * np.cos(angle), weight * np.sin(angle)], axis=1)
    high, low = split_table(last)
    last3 = np.concatenate([high, high, low], axis=1)
    lags = np.concatenate([np.tile(last[4 * sources + part].T, (1, 8)) for part in range(4)], axis=1)
    high, low = split_table(lags)
    lags3 = np.concatenate([high, low, high], axis=0)
    return first3, taps3, twist, second3, last3, lags3


def halves(x):
    high = x.astype(BF16)
    return high, (x - high.astype(F32)).astype(BF16)


def lanes3(x):
    high, low = halves(x)
    return jnp.concatenate([high, low, high], axis=1)


def lanes3_table_last(x):
    high, low = halves(x)
    return jnp.concatenate([high, high, low], axis=1)


def rows3(x):
    high, low = halves(x)
    return jnp.concatenate([high, low, high], axis=0)


def mm(a, b):
    return jnp.dot(a, b, preferred_element_type=F32)


def turned(x_re, x_im, twist_ref):
    cos, sin = twist_ref[0], twist_ref[1]
    return x_re * cos + x_im * sin, x_im * cos - x_re * sin


def second_stage(stacked, second_ref):
    return mm(lanes3_table_last(stacked), second_ref[...])


def lane_group(width, rows):
    return lax.broadcasted_iota(jnp.int32, (rows, 128), 1) // width


def put_places(out_ref, part, row, values):
    start = (part * 8 ^ LEAD_PLACE & 24) * 4 + row
    out_ref[pl.ds(start, 4, stride=4), :] = values[4:]
    out_ref[pl.ds(start + 16, 4, stride=4), :] = values[:4]


def get_places(in_ref, low, row):
    return jnp.concatenate(
        [in_ref[pl.ds((low * 16 + m ^ LEAD_PLACE) * 4 + row, 4, stride=4), :] for m in range(0, 16, 4)], axis=0
    )


def pack_kernel(place_ref, q_ref, k_ref, v_ref, g_ref, f_ref, out_ref):
    gate_in = k_ref[...].astype(F32) * v_ref[...].astype(F32)
    grad_conv = g_ref[...].astype(F32) * q_ref[...].astype(F32)
    for j in range(8):
        cols = slice(j * 128, j * 128 + 128)
        out_ref[pl.ds(j, 16, stride=MSG), :] = gate_in[:, cols]
        out_ref[pl.ds(8 + j, 16, stride=MSG), :] = grad_conv[:, cols]
    for high in range(2):
        flipped = f_ref[:, high * 128 : high * 128 + 128].T
        taps = jnp.concatenate([flipped[m * 16 : m * 16 + 16, :] for m in range(8)], axis=1)
        out_ref[pl.ds(16 + high, 16, stride=MSG), :] = taps


def message_start(block, chan, array):
    return (block * 2 + chan ^ LEAD) * MSG + array * 8


def forward_kernel(in_ref, first_ref, twist_ref, second_ref, lags_ref, spec_ref, out_ref, taps_t, lags_t):
    columns = []
    for array in range(2):
        for chan in range(2):
            starts = [message_start(block, chan, array) for block in range(8)]
            columns.append(jnp.concatenate([in_ref[start : start + 8, :] for start in starts], axis=0))
    signals = jnp.concatenate(columns, axis=1)
    section = mm(first_ref[...], rows3(signals))
    stacked = []
    for s in range(4):
        cols = slice(s * 128, s * 128 + 128)
        re, im = turned(section[:ROWS, cols], section[ROWS:, cols], twist_ref)
        stacked.append(jnp.concatenate([re, im], axis=1))
    spec = second_stage(jnp.concatenate(stacked, axis=0), second_ref)
    spec_ref[...] = spec

    sum_re = jnp.zeros((ROWS, 128), F32)
    sum_im = jnp.zeros((ROWS, 128), F32)
    for chan in range(2):
        x = spec[chan * ROWS : chan * ROWS + ROWS]
        g = spec[(2 + chan) * ROWS : (2 + chan) * ROWS + ROWS]
        sum_re += g[:, :128] * x[:, :128] + g[:, 128:] * x[:, 128:]
        sum_im += g[:, :128] * x[:, 128:] - g[:, 128:] * x[:, :128]
    back = second_stage(jnp.concatenate([sum_re, sum_im], axis=1), second_ref)
    re, im = turned(back[:, :128], back[:, 128:], twist_ref)
    flipped = jnp.concatenate([re, im], axis=0).T
    lags = mm(lanes3_table_last(flipped), lags_ref[...]) * np.float32(1.0 / np.sqrt(32768.0))
    for part in range(4):
        lags_t[part * 128 : part * 128 + 128, :] = lags[:, part * 128 : part * 128 + 128]

    group = lane_group(16, 8)
    zero = jnp.zeros((8, 128), F32)
    for high in range(2):
        taps = in_ref[pl.ds(16 + high, 16, stride=MSG), :]
        taps_t[...] = jnp.concatenate([taps] * 8, axis=0).T
        for b in range(2):
            row = zero
            for a in range(8):
                row = jnp.where(group == a, taps_t[pl.ds(2 * a + b, 8, stride=16), :], row)
            for low in range(2):
                put_places(out_ref, low * 2 + high, b, row)
    for part in range(4):
        for b in range(2):
            row = zero
            for a in range(8):
                row = jnp.where(group == a, lags_t[pl.ds(part * 128 + 2 * a + b, 8, stride=16), :], row)
            put_places(out_ref, part, 2 + b, row)


def backward_kernel(in_ref, spec_ref, taps_ref, twist_ref, second_ref, last_ref, out_ref, taps_t, lags_t):
    group = lane_group(16, 16)
    for b in range(2):
        for low in range(2):
            row = get_places(in_ref, low, b)
            for a in range(8):
                taps_t[pl.ds(low * 256 + 2 * a + b, 16, stride=16), :] = jnp.where(group == a, row, 0.0)
        row = get_places(in_ref, 0, 2 + b) + get_places(in_ref, 1, 2 + b)
        for a in range(8):
            lags_t[pl.ds(2 * a + b, 16, stride=16), :] = jnp.where(group == a, row, 0.0)
    for high in range(2):
        flipped = lags_t[high * 128 : high * 128 + 128, :].T
        total = flipped[:16]
        for a in range(1, 8):
            total += flipped[a * 16 : a * 16 + 16]
        out_ref[pl.ds(16 + high, 16, stride=MSG), :] = total

    taps = jnp.concatenate([lanes3(taps_t[part * 128 : part * 128 + 128, :]) for part in range(4)], axis=1)
    section = lax.dot_general(
        taps_ref[...], taps, (((1,), (1,)), ((), ())), preferred_element_type=F32
    )
    re, im = turned(section[:ROWS], section[ROWS:], twist_ref)
    filt = second_stage(jnp.concatenate([re, im], axis=1), second_ref)
    h_re, h_im = filt[:, :128], filt[:, 128:]

    products = []
    for s in range(4):
        re, im = spec_ref[s * ROWS : s * ROWS + ROWS, :128], spec_ref[s * ROWS : s * ROWS + ROWS, 128:]
        if s < 2:
            products.append(jnp.concatenate([re * h_re - im * h_im, -(re * h_im + im * h_re)], axis=1))
        else:
            products.append(jnp.concatenate([re * h_re + im * h_im, re * h_im - im * h_re], axis=1))
    back = second_stage(jnp.concatenate(products, axis=0), second_ref)
    columns = []
    for s in range(4):
        part = back[s * ROWS : s * ROWS + ROWS]
        re, im = turned(part[:, :128], part[:, 128:], twist_ref)
        columns.append(jnp.concatenate([re, im], axis=0))
    landed = mm(last_ref[...], rows3(jnp.concatenate(columns, axis=1)))
    for s in range(4):
        array, chan = s // 2, s % 2
        for block in range(8):
            start = message_start(block, chan, array)
            out_ref[start : start + 8, :] = landed[block * 8 : block * 8 + 8, s * 128 : s * 128 + 128]


def finish_kernel(in_ref, k_ref, v_ref, g_ref, q_out, k_out, v_out, f_out):
    for j in range(8):
        cols = slice(j * 128, j * 128 + 128)
        conv = in_ref[pl.ds(j, 16, stride=MSG), :]
        grad = in_ref[pl.ds(8 + j, 16, stride=MSG), :]
        q_out[:, cols] = (g_ref[:, cols].astype(F32) * conv).astype(BF16)
        k_out[:, cols] = (grad * v_ref[:, cols].astype(F32)).astype(BF16)
        v_out[:, cols] = (grad * k_ref[:, cols].astype(F32)).astype(BF16)
    for high in range(2):
        flipped = in_ref[pl.ds(16 + high, 16, stride=MSG), :].T
        f_out[:, high * 128 : high * 128 + 128] = jnp.concatenate(
            [flipped[m * 16 : m * 16 + 16, :] for m in range(8)], axis=1
        )


VMEM = pl.BlockSpec(memory_space=pltpu.VMEM)
PARAMS = pltpu.CompilerParams(vmem_limit_bytes=32 * 1024 * 1024)


def shape(*dims, dtype=F32):
    return jax.ShapeDtypeStruct(dims, dtype)


def exchange(rows, axes, count, lead):
    messages = rows.reshape(count, rows.shape[0] // count // 2, 2, 128)
    slots = [slot ^ lead for slot in range(count)]
    arrived = lax.all_to_all(messages, axes, split_axis=0, concat_axis=0, axis_index_groups=[slots], tiled=True)
    return arrived.reshape(rows.shape)


def on_device(q, k, v, filters, g):
    first3, taps3, twist, second3, last3, lags3 = (jnp.asarray(t) for t in tables())
    place = jnp.broadcast_to(lax.axis_index("x").astype(F32), (2048, 128))
    packed = pl.pallas_call(
        pack_kernel,
        out_shape=shape(16 * MSG, 128),
        in_specs=[VMEM] * 6,
        out_specs=VMEM,
        compiler_params=PARAMS,
    )(place, q, k, v, g, filters.T)
    arrived = exchange(packed, ("zh", "x", "zgh"), 16, LEAD)

    spec, sent = pl.pallas_call(
        forward_kernel,
        out_shape=(shape(4 * ROWS, 256), shape(128, 128)),
        in_specs=[VMEM] * 5,
        out_specs=(VMEM, VMEM),
        scratch_shapes=[pltpu.VMEM((128, 128), F32), pltpu.VMEM((512, 128), F32)],
        compiler_params=PARAMS,
    )(arrived, first3, twist, second3, lags3)
    swapped = exchange(sent, ("zgl", "zb", "y", "core"), 32, LEAD_PLACE)

    landed = pl.pallas_call(
        backward_kernel,
        out_shape=shape(16 * MSG, 128),
        in_specs=[VMEM] * 6,
        out_specs=VMEM,
        scratch_shapes=[pltpu.VMEM((512, 128), F32), pltpu.VMEM((256, 128), F32)],
        compiler_params=PARAMS,
    )(swapped, spec, taps3, twist, second3, last3)
    home = exchange(landed, ("zh", "x", "zgh"), 16, LEAD)

    out = shape(*q.shape, dtype=BF16)
    q_grad, k_grad, v_grad, f_grad = pl.pallas_call(
        finish_kernel,
        out_shape=(out, out, out, shape(*filters.shape[::-1])),
        in_specs=[VMEM] * 4,
        out_specs=(VMEM,) * 4,
        compiler_params=PARAMS,
    )(home, k, v, g)
    return q_grad, k_grad, v_grad, f_grad.T


def solution(mesh):
    fine = Mesh(mesh.devices.reshape(2, 4, 2, 2, 2, 4, 2), ("zh", "x", "zgh", "zgl", "zb", "y", "core"))
    seq, chan = ("zh", "x"), ("zgh", "zgl", "zb", "y", "core")
    gates, taps = P(chan, seq), P(None, seq + chan)
    return jax.shard_map(
        on_device,
        mesh=fine,
        in_specs=(gates, gates, gates, taps, gates),
        out_specs=(gates, gates, gates, taps),
        check_vma=False,
    )
```

```python
import ml_dtypes
import numpy as np
import jax
import jax.numpy as jnp
from jax import lax
from jax.experimental import pallas as pl
from jax.experimental.pallas import tpu as pltpu
from jax.sharding import Mesh
from jax.sharding import PartitionSpec as P

N = 16384
ROWS = 72
F32 = jnp.float32
BF16 = jnp.bfloat16
MSG = 18


LEAD = 12
LEAD_PLACE = 20


def split_table(table):
    high = table.astype(ml_dtypes.bfloat16)
    low = (table - high.astype(np.float64)).astype(ml_dtypes.bfloat16)
    return high, low


def tables():
    k1 = np.arange(ROWS)
    live = (k1 <= 64).astype(np.float64)
    t1 = np.arange(64)
    t2 = np.arange(128)
    turn = 2 * np.pi / 128

    angle = turn * (k1[:, None] * t1[None, :] % 128)
    first = np.concatenate([live[:, None] * np.cos(angle), -live[:, None] * np.sin(angle)])
    high, low = split_table(first)
    first2 = np.concatenate([high, low])

    sources = np.arange(16) ^ LEAD
    places = np.concatenate([4 * sources + part for part in range(4)])
    high, low = split_table(first[:, places])
    taps2 = np.concatenate([high, low])

    angle = 2 * np.pi / N * (k1[:, None] * t2[None, :] % N)
    twist = np.stack([live[:, None] * np.cos(angle), live[:, None] * np.sin(angle)]).astype(np.float32)

    angle = turn * (t2[:, None] * t2[None, :] % 128)
    cos, sin = np.cos(angle), np.sin(angle)
    second = np.block([[cos, -sin], [sin, cos]])
    high, low = split_table(second)
    second2 = np.concatenate([high, low])
    mixed = (np.arange(128) % 8) * 16 + np.arange(128) // 8
    both = np.concatenate([mixed, 128 + mixed])
    lags_second = np.concatenate(split_table(second[:, both]))
    taps_second = np.concatenate(split_table(second[both]))
    mixed_twist = twist[:, :, mixed]

    weight = live * np.where((k1 == 0) | (k1 == 64), 1.0, 2.0) / N
    angle = turn * (t1[:, None] * k1[None, :] % 128)
    last = np.concatenate([weight * np.cos(angle), weight * np.sin(angle)], axis=1)
    high, low = split_table(last)
    last2 = np.concatenate([high, low])
    high, low = split_table(last[places])
    lags2 = np.concatenate([high, low])
    return first2, taps2, twist, second2, last2, lags2, mixed_twist, lags_second, taps_second


def halves(x):
    high = x.astype(BF16)
    return high, (x - high.astype(F32)).astype(BF16)


def mm(a, b):
    return jnp.dot(a, b, preferred_element_type=F32)


def turned(x_re, x_im, twist_ref):
    cos, sin = twist_ref[0], twist_ref[1]
    return x_re * cos + x_im * sin, x_im * cos - x_re * sin


def times_data(table_ref, data):
    rows = table_ref.shape[0] // 2
    high, low = halves(data)
    both = mm(table_ref[...], high)
    return both[:rows] + (both[rows:] + mm(table_ref[:rows, :], low))


def second_stage(data, second_ref):
    rows = data.shape[0]
    high, low = halves(data)
    both = mm(jnp.concatenate([high, low], axis=0), second_ref[:256, :])
    return both[:rows] + (both[rows:] + mm(high, second_ref[256:, :]))


def lane_group(width, rows):
    return lax.broadcasted_iota(jnp.int32, (rows, 128), 1) // width


def put_places(out_ref, part, row, values):
    start = (part * 8 ^ LEAD_PLACE & 24) * 4 + row
    out_ref[pl.ds(start, 4, stride=4), :] = values[4:]
    out_ref[pl.ds(start + 16, 4, stride=4), :] = values[:4]


def get_places(in_ref, low, row):
    return jnp.concatenate(
        [in_ref[pl.ds((low * 16 + m ^ LEAD_PLACE) * 4 + row, 4, stride=4), :] for m in range(0, 16, 4)], axis=0
    )


def pack_kernel(place_ref, q_ref, k_ref, v_ref, g_ref, f_ref, out_ref):
    gate_in = k_ref[...].astype(F32) * v_ref[...].astype(F32)
    grad_conv = g_ref[...].astype(F32) * q_ref[...].astype(F32)
    for j in range(8):
        cols = slice(j * 128, j * 128 + 128)
        out_ref[pl.ds(j, 16, stride=MSG), :] = gate_in[:, cols]
        out_ref[pl.ds(8 + j, 16, stride=MSG), :] = grad_conv[:, cols]
    for high in range(2):
        flipped = f_ref[:, high * 128 : high * 128 + 128].T
        taps = jnp.concatenate([flipped[m * 16 : m * 16 + 16, :] for m in range(8)], axis=1)
        out_ref[pl.ds(16 + high, 16, stride=MSG), :] = taps


def message_start(block, chan, array):
    return (block * 2 + chan ^ LEAD) * MSG + array * 8


def spread(values):
    return jnp.concatenate([values] * 8, axis=0).T


def gathered(values):
    flipped = values.T
    total = flipped[:16]
    for a in range(1, 8):
        total += flipped[a * 16 : a * 16 + 16]
    return total


def forward_kernel(
    in_ref, first_ref, twist_ref, second_ref, lags_ref, mixed_ref, lags_second_ref, spec_ref, out_ref, taps_t
):
    columns = []
    for array in range(2):
        for chan in range(2):
            starts = [message_start(block, chan, array) for block in range(8)]
            columns.append(jnp.concatenate([in_ref[start : start + 8, :] for start in starts], axis=0))
    signals = jnp.concatenate(columns, axis=1)
    section = times_data(first_ref, signals)
    stacked = []
    for s in range(4):
        cols = slice(s * 128, s * 128 + 128)
        re, im = turned(section[:ROWS, cols], section[ROWS:, cols], twist_ref)
        stacked.append(jnp.concatenate([re, im], axis=1))
    spec = second_stage(jnp.concatenate(stacked, axis=0), second_ref)
    spec_ref[...] = spec

    sum_re = jnp.zeros((ROWS, 128), F32)
    sum_im = jnp.zeros((ROWS, 128), F32)
    for chan in range(2):
        x = spec[chan * ROWS : chan * ROWS + ROWS]
        g = spec[(2 + chan) * ROWS : (2 + chan) * ROWS + ROWS]
        sum_re += g[:, :128] * x[:, :128] + g[:, 128:] * x[:, 128:]
        sum_im += g[:, :128] * x[:, 128:] - g[:, 128:] * x[:, :128]
    back = second_stage(jnp.concatenate([sum_re, sum_im], axis=1), lags_second_ref)
    re, im = turned(back[:, :128], back[:, 128:], mixed_ref)
    lags = times_data(lags_ref, jnp.concatenate([re, im], axis=0)) * np.float32(1.0 / np.sqrt(32768.0))
    group = lane_group(16, 8)
    zero = jnp.zeros((8, 128), F32)
    for high in range(2):
        taps = in_ref[pl.ds(16 + high, 16, stride=MSG), :]
        taps_t[...] = spread(taps)
        for b in range(2):
            row = zero
            for a in range(8):
                row = jnp.where(group == a, taps_t[pl.ds(2 * a + b, 8, stride=16), :], row)
            for low in range(2):
                put_places(out_ref, low * 2 + high, b, row)
    for part in range(4):
        lags_t = spread(lags[part * 16 : part * 16 + 16])
        for b in range(2):
            row = zero
            for a in range(8):
                start = (2 * a + b) * 8
                row = jnp.where(group == a, lags_t[start : start + 8], row)
            put_places(out_ref, part, 2 + b, row)


def backward_kernel(
    in_ref, spec_ref, taps_ref, twist_ref, second_ref, last_ref, mixed_ref, taps_second_ref, out_ref, lags_t
):
    group = lane_group(16, 16)
    for b in range(2):
        row = get_places(in_ref, 0, 2 + b) + get_places(in_ref, 1, 2 + b)
        for a in range(8):
            lags_t[pl.ds(2 * a + b, 16, stride=16), :] = jnp.where(group == a, row, 0.0)
    for high in range(2):
        out_ref[pl.ds(16 + high, 16, stride=MSG), :] = gathered(lags_t[high * 128 : high * 128 + 128, :])

    parts = []
    for low in range(2):
        rows = [get_places(in_ref, low, b) for b in range(2)]
        for high in range(2):
            pieces = [
                jnp.where(group[:8] == a, rows[b][high * 8 : high * 8 + 8], 0.0) for a in range(8) for b in range(2)
            ]
            parts.append(gathered(jnp.concatenate(pieces, axis=0)))
    taps = jnp.concatenate(parts, axis=0)
    section = times_data(taps_ref, taps)
    re, im = turned(section[:ROWS], section[ROWS:], mixed_ref)
    filt = second_stage(jnp.concatenate([re, im], axis=1), taps_second_ref)
    h_re, h_im = filt[:, :128], filt[:, 128:]

    products = []
    for s in range(4):
        re, im = spec_ref[s * ROWS : s * ROWS + ROWS, :128], spec_ref[s * ROWS : s * ROWS + ROWS, 128:]
        if s < 2:
            products.append(jnp.concatenate([re * h_re - im * h_im, -(re * h_im + im * h_re)], axis=1))
        else:
            products.append(jnp.concatenate([re * h_re + im * h_im, re * h_im - im * h_re], axis=1))
    back = second_stage(jnp.concatenate(products, axis=0), second_ref)
    columns = []
    for s in range(4):
        part = back[s * ROWS : s * ROWS + ROWS]
        re, im = turned(part[:, :128], part[:, 128:], twist_ref)
        columns.append(jnp.concatenate([re, im], axis=0))
    landed = times_data(last_ref, jnp.concatenate(columns, axis=1))
    for s in range(4):
        array, chan = s // 2, s % 2
        for block in range(8):
            start = message_start(block, chan, array)
            out_ref[start : start + 8, :] = landed[block * 8 : block * 8 + 8, s * 128 : s * 128 + 128]


def finish_kernel(in_ref, k_ref, v_ref, g_ref, q_out, k_out, v_out, f_out):
    for j in range(8):
        cols = slice(j * 128, j * 128 + 128)
        conv = in_ref[pl.ds(j, 16, stride=MSG), :]
        grad = in_ref[pl.ds(8 + j, 16, stride=MSG), :]
        q_out[:, cols] = (g_ref[:, cols].astype(F32) * conv).astype(BF16)
        k_out[:, cols] = (grad * v_ref[:, cols].astype(F32)).astype(BF16)
        v_out[:, cols] = (grad * k_ref[:, cols].astype(F32)).astype(BF16)
    for high in range(2):
        flipped = in_ref[pl.ds(16 + high, 16, stride=MSG), :].T
        f_out[:, high * 128 : high * 128 + 128] = jnp.concatenate(
            [flipped[m * 16 : m * 16 + 16, :] for m in range(8)], axis=1
        )


VMEM = pl.BlockSpec(memory_space=pltpu.VMEM)
PARAMS = pltpu.CompilerParams(vmem_limit_bytes=32 * 1024 * 1024)


def shape(*dims, dtype=F32):
    return jax.ShapeDtypeStruct(dims, dtype)


def exchange(rows, axes, count, lead):
    messages = rows.reshape(count, rows.shape[0] // count // 2, 2, 128)
    slots = [slot ^ lead for slot in range(count)]
    arrived = lax.all_to_all(messages, axes, split_axis=0, concat_axis=0, axis_index_groups=[slots], tiled=True)
    return arrived.reshape(rows.shape)


def on_device(q, k, v, filters, g):
    first2, taps2, twist, second2, last2, lags2, mixed_twist, lags_second, taps_second = (
        jnp.asarray(t) for t in tables()
    )
    place = jnp.broadcast_to(lax.axis_index("x").astype(F32), (2048, 128))
    packed = pl.pallas_call(
        pack_kernel,
        out_shape=shape(16 * MSG, 128),
        in_specs=[VMEM] * 6,
        out_specs=VMEM,
        compiler_params=PARAMS,
    )(place, q, k, v, g, filters.T)
    arrived = exchange(packed, ("zh", "x", "zgh"), 16, LEAD)

    spec, sent = pl.pallas_call(
        forward_kernel,
        out_shape=(shape(4 * ROWS, 256), shape(128, 128)),
        in_specs=[VMEM] * 7,
        out_specs=(VMEM, VMEM),
        scratch_shapes=[pltpu.VMEM((128, 128), F32)],
        compiler_params=PARAMS,
    )(arrived, first2, twist, second2, lags2, mixed_twist, lags_second)
    swapped = exchange(sent, ("zgl", "zb", "y", "core"), 32, LEAD_PLACE)

    landed = pl.pallas_call(
        backward_kernel,
        out_shape=shape(16 * MSG, 128),
        in_specs=[VMEM] * 8,
        out_specs=VMEM,
        scratch_shapes=[pltpu.VMEM((256, 128), F32)],
        compiler_params=PARAMS,
    )(swapped, spec, taps2, twist, second2, last2, mixed_twist, taps_second)
    home = exchange(landed, ("zh", "x", "zgh"), 16, LEAD)

    out = shape(*q.shape, dtype=BF16)
    q_grad, k_grad, v_grad, f_grad = pl.pallas_call(
        finish_kernel,
        out_shape=(out, out, out, shape(*filters.shape[::-1])),
        in_specs=[VMEM] * 4,
        out_specs=(VMEM,) * 4,
        compiler_params=PARAMS,
    )(home, k, v, g)
    return q_grad, k_grad, v_grad, f_grad.T


def solution(mesh):
    fine = Mesh(mesh.devices.reshape(2, 4, 2, 2, 2, 4, 2), ("zh", "x", "zgh", "zgl", "zb", "y", "core"))
    seq, chan = ("zh", "x"), ("zgh", "zgl", "zb", "y", "core")
    gates, taps = P(chan, seq), P(None, seq + chan)
    return jax.shard_map(
        on_device,
        mesh=fine,
        in_specs=(gates, gates, gates, taps, gates),
        out_specs=(gates, gates, gates, taps),
        check_vma=False,
    )
```

```python
import ml_dtypes
import numpy as np
import jax
import jax.numpy as jnp
from jax import lax
from jax.experimental import pallas as pl
from jax.experimental.pallas import tpu as pltpu
from jax.sharding import Mesh
from jax.sharding import PartitionSpec as P

N = 16384
ROWS = 72
F32 = jnp.float32
BF16 = jnp.bfloat16
MSG = 18


ORDER = [12, 11, 13, 8, 14, 10, 6, 1, 4, 7, 15, 5, 9, 2, 3, 0]
LEAD_PLACE = 20


def split_table(table):
    high = table.astype(ml_dtypes.bfloat16)
    low = (table - high.astype(np.float64)).astype(ml_dtypes.bfloat16)
    return high, low


def tables():
    k1 = np.arange(ROWS)
    live = (k1 <= 64).astype(np.float64)
    t1 = np.arange(64)
    t2 = np.arange(128)
    turn = 2 * np.pi / 128

    angle = turn * (k1[:, None] * t1[None, :] % 128)
    first = np.concatenate([live[:, None] * np.cos(angle), -live[:, None] * np.sin(angle)])
    high, low = split_table(first)
    first2 = np.concatenate([high, low])

    sources = np.array(ORDER)
    places = np.concatenate([4 * sources + part for part in range(4)])
    high, low = split_table(first[:, places])
    taps2 = np.concatenate([high, low])

    angle = 2 * np.pi / N * (k1[:, None] * t2[None, :] % N)
    twist = np.stack([live[:, None] * np.cos(angle), live[:, None] * np.sin(angle)]).astype(np.float32)

    angle = turn * (t2[:, None] * t2[None, :] % 128)
    cos, sin = np.cos(angle), np.sin(angle)
    second = np.block([[cos, -sin], [sin, cos]])
    high, low = split_table(second)
    second2 = np.concatenate([high, low])
    mixed = (np.arange(128) % 8) * 16 + np.arange(128) // 8
    both = np.concatenate([mixed, 128 + mixed])
    lags_second = np.concatenate(split_table(second[:, both]))
    taps_second = np.concatenate(split_table(second[both]))
    mixed_twist = twist[:, :, mixed]

    weight = live * np.where((k1 == 0) | (k1 == 64), 1.0, 2.0) / N
    angle = turn * (t1[:, None] * k1[None, :] % 128)
    last = np.concatenate([weight * np.cos(angle), weight * np.sin(angle)], axis=1)
    high, low = split_table(last)
    last2 = np.concatenate([high, low])
    high, low = split_table(last[places])
    lags2 = np.concatenate([high, low])
    return first2, taps2, twist, second2, last2, lags2, mixed_twist, lags_second, taps_second


def halves(x):
    high = x.astype(BF16)
    return high, (x - high.astype(F32)).astype(BF16)


def mm(a, b):
    return jnp.dot(a, b, preferred_element_type=F32)


def turned(x_re, x_im, twist_ref):
    cos, sin = twist_ref[0], twist_ref[1]
    return x_re * cos + x_im * sin, x_im * cos - x_re * sin


def times_data(table_ref, data):
    rows = table_ref.shape[0] // 2
    high, low = halves(data)
    both = mm(table_ref[...], high)
    return both[:rows] + (both[rows:] + mm(table_ref[:rows, :], low))


def times_data_once(table_ref, data):
    rows = table_ref.shape[0] // 2
    high, low = halves(data)
    table = jnp.concatenate([table_ref[:rows, :], table_ref[:rows, :], table_ref[rows:, :]], axis=1)
    return mm(table, jnp.concatenate([high, low, high], axis=0))


def second_stage(data, second_ref):
    rows = data.shape[0]
    high, low = halves(data)
    both = mm(jnp.concatenate([high, low], axis=0), second_ref[:256, :])
    return both[:rows] + (both[rows:] + mm(high, second_ref[256:, :]))


def lane_group(width, rows):
    return lax.broadcasted_iota(jnp.int32, (rows, 128), 1) // width


def put_places(out_ref, part, row, values):
    start = (part * 8 ^ LEAD_PLACE & 24) * 4 + row
    out_ref[pl.ds(start, 4, stride=4), :] = values[4:]
    out_ref[pl.ds(start + 16, 4, stride=4), :] = values[:4]


def get_places(in_ref, low, row):
    return jnp.concatenate(
        [in_ref[pl.ds((low * 16 + m ^ LEAD_PLACE) * 4 + row, 4, stride=4), :] for m in range(0, 16, 4)], axis=0
    )


def pack_kernel(place_ref, q_ref, k_ref, v_ref, g_ref, f_ref, out_ref):
    gate_in = k_ref[...].astype(F32) * v_ref[...].astype(F32)
    grad_conv = g_ref[...].astype(F32) * q_ref[...].astype(F32)
    for j in range(8):
        cols = slice(j * 128, j * 128 + 128)
        out_ref[pl.ds(j, 16, stride=MSG), :] = gate_in[:, cols]
        out_ref[pl.ds(8 + j, 16, stride=MSG), :] = grad_conv[:, cols]
    for high in range(2):
        flipped = f_ref[:, high * 128 : high * 128 + 128].T
        taps = jnp.concatenate([flipped[m * 16 : m * 16 + 16, :] for m in range(8)], axis=1)
        out_ref[pl.ds(16 + high, 16, stride=MSG), :] = taps


def message_start(block, chan, array):
    return ORDER.index(block * 2 + chan) * MSG + array * 8


def spread(values):
    return jnp.concatenate([values] * 8, axis=0).T


def gathered(values):
    flipped = values.T
    total = flipped[:16]
    for a in range(1, 8):
        total += flipped[a * 16 : a * 16 + 16]
    return total


def forward_kernel(
    in_ref, first_ref, twist_ref, second_ref, lags_ref, mixed_ref, lags_second_ref, spec_ref, out_ref, taps_t
):
    columns = []
    for array in range(2):
        for chan in range(2):
            starts = [message_start(block, chan, array) for block in range(8)]
            columns.append(jnp.concatenate([in_ref[start : start + 8, :] for start in starts], axis=0))
    signals = jnp.concatenate(columns, axis=1)
    section = times_data_once(first_ref, signals)
    stacked = []
    for s in range(4):
        cols = slice(s * 128, s * 128 + 128)
        re, im = turned(section[:ROWS, cols], section[ROWS:, cols], twist_ref)
        stacked.append(jnp.concatenate([re, im], axis=1))
    spec = second_stage(jnp.concatenate(stacked, axis=0), second_ref)
    spec_ref[...] = spec

    sum_re = jnp.zeros((ROWS, 128), F32)
    sum_im = jnp.zeros((ROWS, 128), F32)
    for chan in range(2):
        x = spec[chan * ROWS : chan * ROWS + ROWS]
        g = spec[(2 + chan) * ROWS : (2 + chan) * ROWS + ROWS]
        sum_re += g[:, :128] * x[:, :128] + g[:, 128:] * x[:, 128:]
        sum_im += g[:, :128] * x[:, 128:] - g[:, 128:] * x[:, :128]
    back = second_stage(jnp.concatenate([sum_re, sum_im], axis=1), lags_second_ref)
    re, im = turned(back[:, :128], back[:, 128:], mixed_ref)
    lags = times_data(lags_ref, jnp.concatenate([re, im], axis=0)) * np.float32(1.0 / np.sqrt(32768.0))
    group = lane_group(16, 8)
    zero = jnp.zeros((8, 128), F32)
    for high in range(2):
        taps = in_ref[pl.ds(16 + high, 16, stride=MSG), :]
        taps_t[...] = spread(taps)
        for b in range(2):
            row = zero
            for a in range(8):
                row = jnp.where(group == a, taps_t[pl.ds(2 * a + b, 8, stride=16), :], row)
            for low in range(2):
                put_places(out_ref, low * 2 + high, b, row)
    for part in range(4):
        lags_t = spread(lags[part * 16 : part * 16 + 16])
        for b in range(2):
            row = zero
            for a in range(8):
                start = (2 * a + b) * 8
                row = jnp.where(group == a, lags_t[start : start + 8], row)
            put_places(out_ref, part, 2 + b, row)


def backward_kernel(
    in_ref, spec_ref, taps_ref, twist_ref, second_ref, last_ref, mixed_ref, taps_second_ref, out_ref, lags_t
):
    group = lane_group(16, 16)
    for b in range(2):
        row = get_places(in_ref, 0, 2 + b) + get_places(in_ref, 1, 2 + b)
        for a in range(8):
            lags_t[pl.ds(2 * a + b, 16, stride=16), :] = jnp.where(group == a, row, 0.0)
    for high in range(2):
        out_ref[pl.ds(16 + high, 16, stride=MSG), :] = gathered(lags_t[high * 128 : high * 128 + 128, :])

    parts = []
    for low in range(2):
        rows = [get_places(in_ref, low, b) for b in range(2)]
        for high in range(2):
            pieces = [
                jnp.where(group[:8] == a, rows[b][high * 8 : high * 8 + 8], 0.0) for a in range(8) for b in range(2)
            ]
            parts.append(gathered(jnp.concatenate(pieces, axis=0)))
    taps = jnp.concatenate(parts, axis=0)
    section = times_data(taps_ref, taps)
    re, im = turned(section[:ROWS], section[ROWS:], mixed_ref)
    filt = second_stage(jnp.concatenate([re, im], axis=1), taps_second_ref)
    h_re, h_im = filt[:, :128], filt[:, 128:]

    products = []
    for s in range(4):
        re, im = spec_ref[s * ROWS : s * ROWS + ROWS, :128], spec_ref[s * ROWS : s * ROWS + ROWS, 128:]
        if s < 2:
            products.append(jnp.concatenate([re * h_re - im * h_im, -(re * h_im + im * h_re)], axis=1))
        else:
            products.append(jnp.concatenate([re * h_re + im * h_im, re * h_im - im * h_re], axis=1))
    back = second_stage(jnp.concatenate(products, axis=0), second_ref)
    columns = []
    for s in range(4):
        part = back[s * ROWS : s * ROWS + ROWS]
        re, im = turned(part[:, :128], part[:, 128:], twist_ref)
        columns.append(jnp.concatenate([re, im], axis=0))
    landed = times_data(last_ref, jnp.concatenate(columns, axis=1))
    for s in range(4):
        array, chan = s // 2, s % 2
        for block in range(8):
            start = message_start(block, chan, array)
            out_ref[start : start + 8, :] = landed[block * 8 : block * 8 + 8, s * 128 : s * 128 + 128]


def finish_kernel(in_ref, k_ref, v_ref, g_ref, q_out, k_out, v_out, f_out):
    for j in range(8):
        cols = slice(j * 128, j * 128 + 128)
        conv = in_ref[pl.ds(j, 16, stride=MSG), :]
        grad = in_ref[pl.ds(8 + j, 16, stride=MSG), :]
        q_out[:, cols] = (g_ref[:, cols].astype(F32) * conv).astype(BF16)
        k_out[:, cols] = (grad * v_ref[:, cols].astype(F32)).astype(BF16)
        v_out[:, cols] = (grad * k_ref[:, cols].astype(F32)).astype(BF16)
    for high in range(2):
        flipped = in_ref[pl.ds(16 + high, 16, stride=MSG), :].T
        f_out[:, high * 128 : high * 128 + 128] = jnp.concatenate(
            [flipped[m * 16 : m * 16 + 16, :] for m in range(8)], axis=1
        )


VMEM = pl.BlockSpec(memory_space=pltpu.VMEM)
PARAMS = pltpu.CompilerParams(vmem_limit_bytes=32 * 1024 * 1024)


def shape(*dims, dtype=F32):
    return jax.ShapeDtypeStruct(dims, dtype)


def exchange(rows, axes, slots):
    messages = rows.reshape(len(slots), rows.shape[0] // len(slots) // 2, 2, 128)
    arrived = lax.all_to_all(messages, axes, split_axis=0, concat_axis=0, axis_index_groups=[slots], tiled=True)
    return arrived.reshape(rows.shape)


def on_device(q, k, v, filters, g):
    first2, taps2, twist, second2, last2, lags2, mixed_twist, lags_second, taps_second = (
        jnp.asarray(t) for t in tables()
    )
    place = jnp.broadcast_to(lax.axis_index("x").astype(F32), (2048, 128))
    packed = pl.pallas_call(
        pack_kernel,
        out_shape=shape(16 * MSG, 128),
        in_specs=[VMEM] * 6,
        out_specs=VMEM,
        compiler_params=PARAMS,
    )(place, q, k, v, g, filters.T)
    arrived = exchange(packed, ("zh", "x", "zgh"), ORDER)

    spec, sent = pl.pallas_call(
        forward_kernel,
        out_shape=(shape(4 * ROWS, 256), shape(128, 128)),
        in_specs=[VMEM] * 7,
        out_specs=(VMEM, VMEM),
        scratch_shapes=[pltpu.VMEM((128, 128), F32)],
        compiler_params=PARAMS,
    )(arrived, first2, twist, second2, lags2, mixed_twist, lags_second)
    swapped = exchange(sent, ("zgl", "zb", "y", "core"), [slot ^ LEAD_PLACE for slot in range(32)])

    landed = pl.pallas_call(
        backward_kernel,
        out_shape=shape(16 * MSG, 128),
        in_specs=[VMEM] * 8,
        out_specs=VMEM,
        scratch_shapes=[pltpu.VMEM((256, 128), F32)],
        compiler_params=PARAMS,
    )(swapped, spec, taps2, twist, second2, last2, mixed_twist, taps_second)
    home = exchange(landed, ("zh", "x", "zgh"), ORDER)

    out = shape(*q.shape, dtype=BF16)
    q_grad, k_grad, v_grad, f_grad = pl.pallas_call(
        finish_kernel,
        out_shape=(out, out, out, shape(*filters.shape[::-1])),
        in_specs=[VMEM] * 4,
        out_specs=(VMEM,) * 4,
        compiler_params=PARAMS,
    )(home, k, v, g)
    return q_grad, k_grad, v_grad, f_grad.T


def solution(mesh):
    fine = Mesh(mesh.devices.reshape(2, 4, 2, 2, 2, 4, 2), ("zh", "x", "zgh", "zgl", "zb", "y", "core"))
    seq, chan = ("zh", "x"), ("zgh", "zgl", "zb", "y", "core")
    gates, taps = P(chan, seq), P(None, seq + chan)
    return jax.shard_map(
        on_device,
        mesh=fine,
        in_specs=(gates, gates, gates, taps, gates),
        out_specs=(gates, gates, gates, taps),
        check_vma=False,
    )
```

```python
import ml_dtypes
import numpy as np
import jax
import jax.numpy as jnp
from jax import lax
from jax.experimental import pallas as pl
from jax.experimental.pallas import tpu as pltpu
from jax.sharding import Mesh
from jax.sharding import PartitionSpec as P

N = 16384
ROWS = 72
F32 = jnp.float32
BF16 = jnp.bfloat16
MSG = 18


ORDER = [12, 11, 13, 8, 14, 10, 15, 1, 4, 7, 6, 5, 9, 2, 3, 0]
LEAD_PLACE = 20


def split_table(table):
    high = table.astype(ml_dtypes.bfloat16)
    low = (table - high.astype(np.float64)).astype(ml_dtypes.bfloat16)
    return high, low


def tables():
    k1 = np.arange(ROWS)
    live = (k1 <= 64).astype(np.float64)
    t1 = np.arange(64)
    t2 = np.arange(128)
    turn = 2 * np.pi / 128

    angle = turn * (k1[:, None] * t1[None, :] % 128)
    first = np.concatenate([live[:, None] * np.cos(angle), -live[:, None] * np.sin(angle)])
    high, low = split_table(first)
    first2 = np.concatenate([high, low])

    sources = np.array(ORDER)
    places = np.concatenate([4 * sources + part for part in range(4)])
    high, low = split_table(first[:, places])
    taps2 = np.concatenate([high, low])

    angle = 2 * np.pi / N * (k1[:, None] * t2[None, :] % N)
    twist = np.stack([live[:, None] * np.cos(angle), live[:, None] * np.sin(angle)]).astype(np.float32)

    angle = turn * (t2[:, None] * t2[None, :] % 128)
    cos, sin = np.cos(angle), np.sin(angle)
    second = np.block([[cos, -sin], [sin, cos]])
    high, low = split_table(second)
    second2 = np.concatenate([high, low])
    mixed = (np.arange(128) % 8) * 16 + np.arange(128) // 8
    both = np.concatenate([mixed, 128 + mixed])
    lags_second = np.concatenate(split_table(second[:, both]))
    taps_second = np.concatenate(split_table(second[both]))
    mixed_twist = twist[:, :, mixed]

    weight = live * np.where((k1 == 0) | (k1 == 64), 1.0, 2.0) / N
    angle = turn * (t1[:, None] * k1[None, :] % 128)
    last = np.concatenate([weight * np.cos(angle), weight * np.sin(angle)], axis=1)
    high, low = split_table(last)
    last2 = np.concatenate([high, low])
    high, low = split_table(last[places])
    lags2 = np.concatenate([high, low])
    return first2, taps2, twist, second2, last2, lags2, mixed_twist, lags_second, taps_second


def halves(x):
    high = x.astype(BF16)
    return high, (x - high.astype(F32)).astype(BF16)


def mm(a, b):
    return jnp.dot(a, b, preferred_element_type=F32)


def turned(x_re, x_im, twist_ref):
    cos, sin = twist_ref[0], twist_ref[1]
    return x_re * cos + x_im * sin, x_im * cos - x_re * sin


def times_data(table_ref, data):
    rows = table_ref.shape[0] // 2
    high, low = halves(data)
    both = mm(table_ref[...], high)
    return both[:rows] + (both[rows:] + mm(table_ref[:rows, :], low))


def times_data_once(table_ref, data):
    rows = table_ref.shape[0] // 2
    high, low = halves(data)
    table = jnp.concatenate([table_ref[:rows, :], table_ref[:rows, :], table_ref[rows:, :]], axis=1)
    return mm(table, jnp.concatenate([high, low, high], axis=0))


def second_stage(data, second_ref):
    rows = data.shape[0]
    high, low = halves(data)
    both = mm(jnp.concatenate([high, low], axis=0), second_ref[:256, :])
    return both[:rows] + (both[rows:] + mm(high, second_ref[256:, :]))


def lane_group(width, rows):
    return lax.broadcasted_iota(jnp.int32, (rows, 128), 1) // width


def put_places(out_ref, part, row, values):
    start = (part * 8 ^ LEAD_PLACE & 24) * 4 + row
    out_ref[pl.ds(start, 4, stride=4), :] = values[4:]
    out_ref[pl.ds(start + 16, 4, stride=4), :] = values[:4]


def get_places(in_ref, low, row):
    return jnp.concatenate(
        [in_ref[pl.ds((low * 16 + m ^ LEAD_PLACE) * 4 + row, 4, stride=4), :] for m in range(0, 16, 4)], axis=0
    )


def pack_kernel(place_ref, q_ref, k_ref, v_ref, g_ref, f_ref, out_ref):
    gate_in = k_ref[...].astype(F32) * v_ref[...].astype(F32)
    grad_conv = g_ref[...].astype(F32) * q_ref[...].astype(F32)
    for j in range(8):
        cols = slice(j * 128, j * 128 + 128)
        out_ref[pl.ds(j, 16, stride=MSG), :] = gate_in[:, cols]
        out_ref[pl.ds(8 + j, 16, stride=MSG), :] = grad_conv[:, cols]
    for high in range(2):
        flipped = f_ref[:, high * 128 : high * 128 + 128].T
        taps = jnp.concatenate([flipped[m * 16 : m * 16 + 16, :] for m in range(8)], axis=1)
        out_ref[pl.ds(16 + high, 16, stride=MSG), :] = taps


def message_start(block, chan, array):
    return ORDER.index(block * 2 + chan) * MSG + array * 8


def spread(values):
    return jnp.concatenate([values] * 8, axis=0).T


def gathered(values):
    flipped = values.T
    total = flipped[:16]
    for a in range(1, 8):
        total += flipped[a * 16 : a * 16 + 16]
    return total


def forward_kernel(
    in_ref, first_ref, twist_ref, second_ref, lags_ref, mixed_ref, lags_second_ref, spec_ref, out_ref, taps_t
):
    columns = []
    for array in range(2):
        for chan in range(2):
            starts = [message_start(block, chan, array) for block in range(8)]
            columns.append(jnp.concatenate([in_ref[start : start + 8, :] for start in starts], axis=0))
    signals = jnp.concatenate(columns, axis=1)
    section = times_data_once(first_ref, signals)
    stacked = []
    for s in range(4):
        cols = slice(s * 128, s * 128 + 128)
        re, im = turned(section[:ROWS, cols], section[ROWS:, cols], twist_ref)
        stacked.append(jnp.concatenate([re, im], axis=1))
    spec = second_stage(jnp.concatenate(stacked, axis=0), second_ref)
    spec_ref[...] = spec

    sum_re = jnp.zeros((ROWS, 128), F32)
    sum_im = jnp.zeros((ROWS, 128), F32)
    for chan in range(2):
        x = spec[chan * ROWS : chan * ROWS + ROWS]
        g = spec[(2 + chan) * ROWS : (2 + chan) * ROWS + ROWS]
        sum_re += g[:, :128] * x[:, :128] + g[:, 128:] * x[:, 128:]
        sum_im += g[:, :128] * x[:, 128:] - g[:, 128:] * x[:, :128]
    back = second_stage(jnp.concatenate([sum_re, sum_im], axis=1), lags_second_ref)
    re, im = turned(back[:, :128], back[:, 128:], mixed_ref)
    lags = times_data(lags_ref, jnp.concatenate([re, im], axis=0)) * np.float32(1.0 / np.sqrt(32768.0))
    group = lane_group(16, 8)
    zero = jnp.zeros((8, 128), F32)
    for high in range(2):
        taps = in_ref[pl.ds(16 + high, 16, stride=MSG), :]
        taps_t[...] = spread(taps)
        for b in range(2):
            row = zero
            for a in range(8):
                row = jnp.where(group == a, taps_t[pl.ds(2 * a + b, 8, stride=16), :], row)
            for low in range(2):
                put_places(out_ref, low * 2 + high, b, row)
    for part in range(4):
        lags_t = spread(lags[part * 16 : part * 16 + 16])
        for b in range(2):
            row = zero
            for a in range(8):
                start = (2 * a + b) * 8
                row = jnp.where(group == a, lags_t[start : start + 8], row)
            put_places(out_ref, part, 2 + b, row)


def backward_kernel(
    in_ref, spec_ref, taps_ref, twist_ref, second_ref, last_ref, mixed_ref, taps_second_ref, out_ref, lags_t
):
    group = lane_group(16, 16)
    for b in range(2):
        row = get_places(in_ref, 0, 2 + b) + get_places(in_ref, 1, 2 + b)
        for a in range(8):
            lags_t[pl.ds(2 * a + b, 16, stride=16), :] = jnp.where(group == a, row, 0.0)
    for high in range(2):
        out_ref[pl.ds(16 + high, 16, stride=MSG), :] = gathered(lags_t[high * 128 : high * 128 + 128, :])

    parts = []
    for low in range(2):
        rows = [get_places(in_ref, low, b) for b in range(2)]
        for high in range(2):
            pieces = [
                jnp.where(group[:8] == a, rows[b][high * 8 : high * 8 + 8], 0.0) for a in range(8) for b in range(2)
            ]
            parts.append(gathered(jnp.concatenate(pieces, axis=0)))
    taps = jnp.concatenate(parts, axis=0)
    section = times_data(taps_ref, taps)
    re, im = turned(section[:ROWS], section[ROWS:], mixed_ref)
    filt = second_stage(jnp.concatenate([re, im], axis=1), taps_second_ref)
    h_re, h_im = filt[:, :128], filt[:, 128:]

    products = []
    for s in range(4):
        re, im = spec_ref[s * ROWS : s * ROWS + ROWS, :128], spec_ref[s * ROWS : s * ROWS + ROWS, 128:]
        if s < 2:
            products.append(jnp.concatenate([re * h_re - im * h_im, -(re * h_im + im * h_re)], axis=1))
        else:
            products.append(jnp.concatenate([re * h_re + im * h_im, re * h_im - im * h_re], axis=1))
    back = second_stage(jnp.concatenate(products, axis=0), second_ref)
    columns = []
    for s in range(4):
        part = back[s * ROWS : s * ROWS + ROWS]
        re, im = turned(part[:, :128], part[:, 128:], twist_ref)
        columns.append(jnp.concatenate([re, im], axis=0))
    landed = times_data(last_ref, jnp.concatenate(columns, axis=1))
    for s in range(4):
        array, chan = s // 2, s % 2
        for block in range(8):
            start = message_start(block, chan, array)
            out_ref[start : start + 8, :] = landed[block * 8 : block * 8 + 8, s * 128 : s * 128 + 128]


def finish_kernel(in_ref, k_ref, v_ref, g_ref, q_out, k_out, v_out, f_out):
    for j in range(8):
        cols = slice(j * 128, j * 128 + 128)
        conv = in_ref[pl.ds(j, 16, stride=MSG), :]
        grad = in_ref[pl.ds(8 + j, 16, stride=MSG), :]
        q_out[:, cols] = (g_ref[:, cols].astype(F32) * conv).astype(BF16)
        k_out[:, cols] = (grad * v_ref[:, cols].astype(F32)).astype(BF16)
        v_out[:, cols] = (grad * k_ref[:, cols].astype(F32)).astype(BF16)
    for high in range(2):
        flipped = in_ref[pl.ds(16 + high, 16, stride=MSG), :].T
        f_out[:, high * 128 : high * 128 + 128] = jnp.concatenate(
            [flipped[m * 16 : m * 16 + 16, :] for m in range(8)], axis=1
        )


VMEM = pl.BlockSpec(memory_space=pltpu.VMEM)
PARAMS = pltpu.CompilerParams(vmem_limit_bytes=32 * 1024 * 1024)


def shape(*dims, dtype=F32):
    return jax.ShapeDtypeStruct(dims, dtype)


def exchange(rows, axes, slots):
    messages = rows.reshape(len(slots), rows.shape[0] // len(slots) // 2, 2, 128)
    arrived = lax.all_to_all(messages, axes, split_axis=0, concat_axis=0, axis_index_groups=[slots], tiled=True)
    return arrived.reshape(rows.shape)


def on_device(q, k, v, filters, g):
    first2, taps2, twist, second2, last2, lags2, mixed_twist, lags_second, taps_second = (
        jnp.asarray(t) for t in tables()
    )
    place = jnp.broadcast_to(lax.axis_index("x").astype(F32), (2048, 128))
    packed = pl.pallas_call(
        pack_kernel,
        out_shape=shape(16 * MSG, 128),
        in_specs=[VMEM] * 6,
        out_specs=VMEM,
        compiler_params=PARAMS,
    )(place, q, k, v, g, filters.T)
    arrived = exchange(packed, ("zh", "x", "zgh"), ORDER)

    spec, sent = pl.pallas_call(
        forward_kernel,
        out_shape=(shape(4 * ROWS, 256), shape(128, 128)),
        in_specs=[VMEM] * 7,
        out_specs=(VMEM, VMEM),
        scratch_shapes=[pltpu.VMEM((128, 128), F32)],
        compiler_params=PARAMS,
    )(arrived, first2, twist, second2, lags2, mixed_twist, lags_second)
    swapped = exchange(sent, ("zgl", "zb", "y", "core"), [slot ^ LEAD_PLACE for slot in range(32)])

    landed = pl.pallas_call(
        backward_kernel,
        out_shape=shape(16 * MSG, 128),
        in_specs=[VMEM] * 8,
        out_specs=VMEM,
        scratch_shapes=[pltpu.VMEM((256, 128), F32)],
        compiler_params=PARAMS,
    )(swapped, spec, taps2, twist, second2, last2, mixed_twist, taps_second)
    home = exchange(landed, ("zh", "x", "zgh"), ORDER)

    out = shape(*q.shape, dtype=BF16)
    q_grad, k_grad, v_grad, f_grad = pl.pallas_call(
        finish_kernel,
        out_shape=(out, out, out, shape(*filters.shape[::-1])),
        in_specs=[VMEM] * 4,
        out_specs=(VMEM,) * 4,
        compiler_params=PARAMS,
    )(home, k, v, g)
    return q_grad, k_grad, v_grad, f_grad.T


def solution(mesh):
    fine = Mesh(mesh.devices.reshape(2, 4, 2, 2, 2, 4, 2), ("zh", "x", "zgh", "zgl", "zb", "y", "core"))
    seq, chan = ("zh", "x"), ("zgh", "zgl", "zb", "y", "core")
    gates, taps = P(chan, seq), P(None, seq + chan)
    return jax.shard_map(
        on_device,
        mesh=fine,
        in_specs=(gates, gates, gates, taps, gates),
        out_specs=(gates, gates, gates, taps),
        check_vma=False,
    )
```
